1024 devices in a mesh: grp: 16 (over y_hi, x, core), fsdp: 64 (over z, y_lo).
Axes of the slice: x: 4, y: 8 (y_hi: 2, y_lo: 4; y = y_hi * 4 + y_lo), z: 16, core: 2. Of those that a mesh axis runs over, the one named last changes fastest.
Arguments:
- tokens: bfloat16 [262144, 768], P(('grp', 'fsdp')), may hold values from -6 to 6
- send_order: int32 [1024, 256], P(('grp', 'fsdp')), may hold values from 0 to 255, each once within a row
- recv_order: int32 [1024, 256], P(('grp', 'fsdp')), may hold values from 0 to 255, each once within a row
- row_ids: int32 [1024, 256], P(('grp', 'fsdp')), may hold values from 0 to 3, never falling along the last dimension, each value on 1 to 128 neighbouring positions
- frames: int32 [1024, 4], P(('grp', 'fsdp')), may hold values from 0 to 128
- norm_scale: float32 [2, 768], replicated, may hold values from 0.5 to 1.5
- norm_shift: float32 [2, 768], replicated, may hold values from -3 to 3
- qkv_weight: bfloat16 [768, 1152], P('fsdp'), may hold values from -0.21875 to 0.21875
- d_out: bfloat16 [262144, 384], P(('grp', 'fsdp')), may hold values from -6 to 6
Outputs:
- attended: bfloat16 [262144, 384], P(('grp', 'fsdp'))
- grad_tokens: bfloat16 [262144, 768], P(('grp', 'fsdp'))
- grad_weight: float32 [768, 1152], P('fsdp', 'grp')
- grad_scale: float32 [2, 768], replicated
- grad_shift: float32 [2, 768], replicated
The draws below stay inside these ranges and needn't reach their ends.
All inputs are finite; a program needn't handle non-finite values.
Results may differ from the reference program's by a relative error of at most 0.02.
Values may be sent and summed in bfloat16 or wider, within the bound.
A program may use at most 32 MiB of HBM per device.

```python
import math
import jax
import jax.numpy as jnp
import numpy as np
from jax import lax

D = 768
HEADS = 6
HEAD_DIM = 64
TOK_DEV = 256
SEGS = 4
ROW_MOST = 128
INNER = 384
TRIPLE = 1152
TOKENS = 262144
N_GRP = 16
N_FSDP = 64


def with_ends(entries, own_key, least, largest):
    longest = entries.shape.index(max(entries.shape))
    spots = []
    for shift in (0, 1):
        where = [jax.random.randint(jax.random.fold_in(own_key, axis), (), 0, length) for axis, length in enumerate(entries.shape)]
        where[longest] = (where[longest] + shift) % entries.shape[longest]
        spots.append(tuple(where))
    return entries.at[spots[0]].set(least).at[spots[1]].set(largest)


def level_of(rng, shape, pieces, low, top_value):
    level, own = 1.0, jax.random.fold_in(rng, 6)
    for dim, parts in pieces:
        heights = jnp.exp(jax.random.uniform(jax.random.fold_in(own, dim), (parts,), jnp.float32, low / len(pieces), top_value / len(pieces)))
        level = level * jnp.repeat(heights, shape[dim] // parts).reshape([-1 if axis == dim else 1 for axis in range(len(shape))])
    return level


def length_profile(count, total, reach, lean):
    loads = [(1 << 20) // math.isqrt(rank ** lean) + 1 for rank in range(2, count + 1)]
    spare, counts = total - reach - (count - 1), [1] * (count - 1)
    while spare > 0:
        movable = [i for i in range(count - 1) if counts[i] < reach]
        mass, left = sum([loads[i] for i in movable]), spare
        for i in movable:
            extra = min(reach - counts[i], max(1, left * loads[i] // mass), spare)
            counts[i] = counts[i] + extra
            spare = spare - extra
    return np.array([reach] + counts)


def uneven(rng, count, total, most, slope):
    if count == 2:
        one = jax.random.randint(rng, (), max(1, total - most), min(most, total - 1) + 1)
        return jnp.stack([one, total - one])
    tallies = jnp.asarray(length_profile(count, total, most, slope), jnp.int32)
    pairs = (count - 1) // 2
    giver, sink = tallies[1:1 + 2 * pairs:2], tallies[2:2 + 2 * pairs:2]
    slack = jnp.minimum(giver - 1, most - sink)
    passed = jax.random.randint(jax.random.fold_in(rng, 1), (pairs,), 0, 1 << 20) % (slack + 1)
    tallies = tallies.at[1:1 + 2 * pairs:2].set(giver - passed).at[2:2 + 2 * pairs:2].set(sink + passed)
    return tallies[jax.random.permutation(jax.random.fold_in(rng, 2), count)]


def scatter_about(stream_key, shape, spread, bound, shards=(), held_as=jnp.bfloat16):
    array = spread * jax.random.normal(stream_key, shape, jnp.float32)
    if shards:
        array = array * level_of(stream_key, shape, shards, -0.22, 0.18)
    return jnp.clip(array, -bound, bound).astype(held_as)


def setup_inputs(seed: int = 0) -> dict:
    key_of = jax.random.split(jax.random.key(seed), 10)
    tokens = scatter_about(key_of[0], (TOKENS, D), 1.0, 6.0, ((0, 1024),))
    send_order = jax.vmap(lambda own: jax.random.permutation(own, TOK_DEV))(jax.random.split(key_of[1], (N_GRP * N_FSDP))).reshape((N_GRP * N_FSDP, TOK_DEV)).astype(jnp.int32)
    recv_order = jax.vmap(lambda own: jax.random.permutation(own, TOK_DEV))(jax.random.split(key_of[2], (N_GRP * N_FSDP))).reshape((N_GRP * N_FSDP, TOK_DEV)).astype(jnp.int32)
    row_ids = jax.vmap(lambda own: jnp.searchsorted(jnp.cumsum(uneven(own, SEGS, TOK_DEV, ROW_MOST, 2)), jnp.arange(TOK_DEV), side="right"))(jax.random.split(key_of[3], (N_GRP * N_FSDP))).reshape((N_GRP * N_FSDP, TOK_DEV)).astype(jnp.int32)
    frames = with_ends(jax.random.randint(key_of[4], (N_GRP * N_FSDP, SEGS), 0, ROW_MOST + 1), jax.random.fold_in(key_of[4], 1), 0, ROW_MOST).astype(jnp.int32)
    norm_scale = jnp.clip(jax.random.uniform(key_of[5], (2, D), jnp.float32, 0.5, 1.5), 0.5, 1.5)
    norm_shift = scatter_about(key_of[6], (2, D), 0.5, 3.0, (), jnp.float32)
    qkv_weight = scatter_about(key_of[7], (D, TRIPLE), D ** -0.5, 0.21875, ((0, 64),))
    d_out = scatter_about(key_of[8], (TOKENS, INNER), 1.0, 6.0, ((0, 1024),))
    return {"tokens": tokens, "send_order": send_order, "recv_order": recv_order, "row_ids": row_ids, "frames": frames, "norm_scale": norm_scale, "norm_shift": norm_shift, "qkv_weight": qkv_weight, "d_out": d_out}


epsilon = 1e-06

def audio_flags(row_ids, frames):
    position = jnp.arange(row_ids.shape[0], dtype=jnp.int32)
    before = lax.optimization_barrier(jnp.sum((row_ids[None, :] < row_ids[:, None]).astype(jnp.int32), axis=1))
    place = position - before
    one_hot = row_ids[:, None] == jnp.arange(frames.shape[0], dtype=jnp.int32)[None, :]
    video_limit = lax.optimization_barrier(jnp.sum(jnp.where(one_hot, frames[None, :], 0), axis=1))
    return place >= video_limit

def device_pass(packed, row_ids, frames, norm_scale, norm_shift, weight, grad_out):
    slot_count = packed.shape[0]
    values_f32 = packed.astype(jnp.float32)
    average = lax.optimization_barrier(jnp.mean(values_f32, axis=1, keepdims=True))
    centered = values_f32 - average
    variance = lax.optimization_barrier(jnp.mean(centered * centered, axis=1, keepdims=True))
    inverse_std = lax.rsqrt(variance + epsilon)
    standard = centered * inverse_std
    is_audio = audio_flags(row_ids, frames)[:, None]
    row_gain = jnp.where(is_audio, norm_scale[1][None, :], norm_scale[0][None, :])
    row_bias = jnp.where(is_audio, norm_shift[1][None, :], norm_shift[0][None, :])
    normalized = (standard * row_gain + row_bias).astype(jnp.bfloat16)
    qkv = jnp.dot(normalized, weight, preferred_element_type=jnp.float32).astype(jnp.bfloat16)
    inner = HEADS * HEAD_DIM
    query_rows = qkv[:, :inner].reshape(slot_count, HEADS, HEAD_DIM).astype(jnp.float32)
    key_rows = qkv[:, inner:2 * inner].reshape(slot_count, HEADS, HEAD_DIM).astype(jnp.float32)
    value_rows = qkv[:, 2 * inner:].reshape(slot_count, HEADS, HEAD_DIM).astype(jnp.float32)
    scaling = 1.0 / HEAD_DIM ** 0.5
    scores = jnp.einsum('qhd,khd->hqk', query_rows, key_rows) * scaling
    same_row = (row_ids[:, None] == row_ids[None, :])[None, :, :]
    scores = jnp.where(same_row, scores, -1e+30)
    peak = lax.optimization_barrier(jnp.max(scores, axis=2, keepdims=True))
    exponent = jnp.exp(scores - peak)
    attn_probs = (exponent / lax.optimization_barrier(jnp.sum(exponent, axis=2, keepdims=True))).astype(jnp.bfloat16)
    probs_f32 = attn_probs.astype(jnp.float32)
    attended = jnp.einsum('hqk,khd->qhd', probs_f32, value_rows).reshape(slot_count, inner).astype(jnp.bfloat16)
    grad_heads = grad_out.reshape(slot_count, HEADS, HEAD_DIM).astype(jnp.float32)
    grad_probs = jnp.einsum('qhd,khd->hqk', grad_heads, value_rows)
    row_delta = lax.optimization_barrier(jnp.sum(grad_heads * attended.reshape(slot_count, HEADS, HEAD_DIM).astype(jnp.float32), axis=2))
    grad_scores = (probs_f32 * (grad_probs - jnp.transpose(row_delta)[:, :, None]) * scaling).astype(jnp.bfloat16)
    grad_scores = grad_scores.astype(jnp.float32)
    grad_query = jnp.einsum('hqk,khd->qhd', grad_scores, key_rows).reshape(slot_count, inner)
    grad_key = jnp.einsum('hqk,qhd->khd', grad_scores, query_rows).reshape(slot_count, inner)
    grad_value = jnp.einsum('hqk,qhd->khd', probs_f32, grad_heads).reshape(slot_count, inner)
    grad_qkv = jnp.concatenate([grad_query, grad_key, grad_value], axis=1).astype(jnp.bfloat16)
    weight_term = lax.dot_general(normalized, grad_qkv, (((0,), (0,)), ((), ())), preferred_element_type=jnp.float32)
    grad_normed = lax.dot_general(grad_qkv, weight, (((1,), (1,)), ((), ())), preferred_element_type=jnp.float32)
    gain_term = grad_normed * standard
    scale_term = jnp.stack([lax.optimization_barrier(jnp.sum(jnp.where(is_audio, 0.0, gain_term), axis=0)), lax.optimization_barrier(jnp.sum(jnp.where(is_audio, gain_term, 0.0), axis=0))])
    shift_term = jnp.stack([lax.optimization_barrier(jnp.sum(jnp.where(is_audio, 0.0, grad_normed), axis=0)), lax.optimization_barrier(jnp.sum(jnp.where(is_audio, grad_normed, 0.0), axis=0))])
    scaled = grad_normed * row_gain
    grad_packed = inverse_std * (scaled - lax.optimization_barrier(jnp.mean(scaled, axis=1, keepdims=True)) - standard * lax.optimization_barrier(jnp.mean(scaled * standard, axis=1, keepdims=True)))
    return (attended, grad_packed.astype(jnp.bfloat16), weight_term, scale_term, shift_term)

def reference(tokens, send_order, recv_order, row_ids, frames, norm_scale, norm_shift, qkv_weight, d_out):
    per_peer = TOK_DEV // N_FSDP

    def move(flat):
        grid = flat.reshape(N_GRP, N_FSDP, TOK_DEV, D)
        sent = jnp.take_along_axis(grid, send_order.reshape(N_GRP, N_FSDP, TOK_DEV)[..., None], axis=2)
        arrived = sent.reshape(N_GRP, N_FSDP, N_FSDP, per_peer, D).transpose(0, 2, 1, 3, 4).reshape(N_GRP, N_FSDP, TOK_DEV, D)
        packed_grid = jnp.take_along_axis(arrived, recv_order.reshape(N_GRP, N_FSDP, TOK_DEV)[..., None], axis=2)
        return packed_grid.reshape(N_GRP * N_FSDP, TOK_DEV, D)
    packed, move_back = jax.vjp(move, tokens)
    grad_rows = d_out.reshape(N_GRP * N_FSDP, TOK_DEV, HEADS * HEAD_DIM)

    def visit(carry, inputs):
        packed_dev, rows_dev, frames_dev, grad_dev = inputs
        attended, grad_packed, weight_term, scale_term, shift_term = device_pass(packed_dev, rows_dev, frames_dev, norm_scale, norm_shift, qkv_weight, grad_dev)
        return ((carry[0] + weight_term, carry[1] + scale_term, carry[2] + shift_term), (attended, grad_packed))
    start = (jnp.zeros((D, 3 * HEADS * HEAD_DIM), jnp.float32), jnp.zeros((2, D), jnp.float32), jnp.zeros((2, D), jnp.float32))
    totals, outputs = lax.scan(visit, start, (packed, row_ids, frames, grad_rows))
    attended_all = outputs[0].reshape(TOK_DEV * N_GRP * N_FSDP, HEADS * HEAD_DIM)
    grad_tokens = move_back(outputs[1])[0]
    return (attended_all, grad_tokens, totals[0], totals[1], totals[2])
```

```python
import functools

import jax
import jax.numpy as jnp
import numpy as np
from jax import lax
from jax.experimental import pallas as pl
from jax.experimental.pallas import tpu as pltpu
from jax.sharding import PartitionSpec as P

HEAD_DIM = 64
EPSILON = 1e-06
MESH = pl.DeviceIdType.MESH
BF16 = jnp.bfloat16
F32 = jnp.float32
ROWS16 = 16
ROWS8 = 8
LANES = 128
CHUNKS = 3


class Sizes:
    def __init__(self, grp, fsdp, slots, width, columns):
        self.yh, self.x, self.c = {16: (2, 4, 2), 4: (1, 2, 2), 8: (2, 2, 2)}[grp]
        self.yl = 4 if fsdp == 64 else 2
        self.z = fsdp // self.yl
        self.zb = 4 if self.z == 16 else 2
        self.za = self.z // self.zb
        self.y = self.yh * self.yl
        self.slots, self.width, self.columns = slots, width, columns
        self.inner = columns // 3
        self.per_peer = slots // fsdp
        self.rows = width // fsdp
        self.half_rows = self.rows // 2
        self.col_block = columns // grp
        self.chip_block = self.col_block * self.c
        self.pieces = self.yh * self.x
        self.chunk = width // CHUNKS
        self.half = width // 2
        self.z_lanes = self.z * self.half_rows


def index_rows(s):
    table = np.full((8, max(s.width, s.yl * LANES, s.slots)), -1, np.int32)
    for j in range(s.width):
        h, r = divmod(j, s.half)
        yl, r = divmod(r, s.z_lanes)
        z, i = divmod(r, s.half_rows)
        table[0, j] = (z * s.yl + yl) * s.rows + h * s.half_rows + i
    for yl in range(s.yl):
        for j in range(s.z_lanes):
            table[1, yl * LANES + j] = yl * s.z_lanes + j
    for yl in range(s.yl):
        for z in range(s.z):
            for r in range(s.per_peer):
                q = (yl * s.z + z) * s.per_peer + r
                table[2, q] = (z * s.yl + yl) * s.per_peer + r
    for yl in range(s.yl):
        for i in range(s.rows):
            table[3, yl * ROWS16 + i] = yl * s.rows + i
    for z in range(s.z):
        for i in range(s.half_rows):
            table[4, z * s.half_rows + i] = z * ROWS8 + i
    return table


def one_hot(count, row):
    ids = lax.broadcasted_iota(jnp.int32, (count, row.shape[1]), 0)
    return jnp.where(ids == row, 1.0, 0.0).astype(BF16)


def mm(a, b, dims=((1,), (0,))):
    return lax.dot_general(a, b, (dims, ((), ())), preferred_element_type=F32)


TN = ((0,), (0,))
NT = ((1,), (1,))


def kernel(
    s, tok, send_order, recv_order, row_ids, frames, gains, biases, wshard, dout, table,
    attended, grad_tokens, grad_weight, grad_scale, grad_shift,
    pt, perm, rt, feat, a_out, a_in, b_out, b_in, packed, wpad, wsh, wyin, weight,
    aud, standard, inv, normed, normed_p, qkv, gqkv, gnorm, gpacked,
    r_out, r_in, t_out, t_in, g_send, g_own, g_in, x_out, x_in, y_out, y_in, z_out, z_in,
    f_send, f_in, n_c, n_x, n_y, n_zb, n_za,
    ya_s, ya_r, za_s, za_r, yb_s, yb_r, zb_s, zb_r,
    wz_s, wz_r, wy_s, wy_r, wx_s, wx_r, wc_s, wc_r,
    gc_s, gc_r, gx_s, gx_r, gy_s, gy_r, gz_s, gz_r, gf_s, gf_r,
    nc_s, nc_r, nx_s, nx_r, ny_s, ny_r, nzb_s, nzb_r, nza_s, nza_r,
):
    g = lax.axis_index("grp")
    f = lax.axis_index("fsdp")
    core = g % s.c
    my_x = (g // s.c) % s.x
    my_yh = g // (s.c * s.x)
    my_z = f // s.yl
    my_yl = f % s.yl
    my_y = my_yh * s.yl + my_yl
    other = 1 - core

    def grp_of(yh, x, c):
        return (yh * s.x + x) * s.c + c

    def at_z(z):
        return (g, z * s.yl + my_yl)

    def at_yl(yl):
        return (g, my_z * s.yl + yl)

    def at_y(y):
        return (grp_of(y // s.yl, my_x, core), my_z * s.yl + y % s.yl)

    def at_x(x):
        return (grp_of(my_yh, x, core), f)

    sibling = (grp_of(my_yh, my_x, other), f)

    def others(count, me, body):
        def step(k, carry):
            body((me + k) % count)
            return carry

        lax.fori_loop(1, count, step, 0)

    def remote(src, dst, send, recv, device):
        return pltpu.make_async_remote_copy(
            src_ref=src, dst_ref=dst, send_sem=send, recv_sem=recv,
            device_id=device, device_id_type=MESH,
        )

    barrier = pltpu.get_barrier_semaphore()

    def greet(device):
        pl.semaphore_signal(barrier, inc=1, device_id=device, device_id_type=MESH)

    others(s.z, my_z, lambda z: greet(at_z(z)))
    others(s.y, my_y, lambda y: greet(at_y(y)))
    others(s.x, my_x, lambda x: greet(at_x(x)))
    greet(sibling)

    to_q = one_hot(s.slots, table[2:3, : s.slots])
    perm[...] = to_q
    pt[...] = mm(one_hot(s.slots, send_order[...]), to_q).astype(BF16)
    rt[...] = one_hot(s.slots, recv_order[...])
    wpad[...] = jnp.zeros_like(wpad)
    wpad[0 : s.rows, :] = wshard[...]
    for c in range(CHUNKS):
        a_out[c] = mm(pt[...], tok[:, c * s.chunk : (c + 1) * s.chunk], TN).astype(BF16)
    pl.semaphore_wait(barrier, (s.z - 1) + (s.y - 1) + (s.x - 1) + 1)

    @pl.when(my_z == g)
    def _():
        def send(z):
            remote(wpad, wsh, wz_s.at[z], wz_r.at[0], at_z(z)).start()

        others(s.z, my_z, send)
        wsh[...] = wpad[...]

    run = s.slots // s.yl
    block = s.slots // s.z

    def q_rows(yl):
        return pl.ds(pl.multiple_of(yl * run, run), run)

    def s_rows(z):
        return pl.ds(pl.multiple_of(z * block, block), block)

    def y_copy(out, into, send, recv, c, yl, slot):
        return remote(
            out.at[c, q_rows(yl), :], into.at[c, q_rows(slot), :],
            send.at[c * s.yl + yl], recv.at[c * s.yl + slot], at_yl(yl),
        )

    def z_copy(out, into, send, recv, c, z, slot):
        return remote(
            out.at[c, s_rows(z), :], into.at[c, s_rows(slot), :],
            send.at[c * s.z + z], recv.at[c * s.z + slot], at_z(z),
        )

    def y_start(out, into, send, recv, c):
        others(s.yl, my_yl, lambda y: y_copy(out, into, send, recv, c, y, my_yl).start())
        into[c, q_rows(my_yl), :] = out[c, q_rows(my_yl), :]

    def y_wait(out, into, send, recv, c):
        others(s.yl, my_yl, lambda y: y_copy(out, into, send, recv, c, y, y).wait_recv())

    def z_start(out, into, send, recv, c):
        others(s.z, my_z, lambda z: z_copy(out, into, send, recv, c, z, my_z).start())
        into[c, s_rows(my_z), :] = out[c, s_rows(my_z), :]

    def z_wait(out, into, send, recv, c):
        others(s.z, my_z, lambda z: z_copy(out, into, send, recv, c, z, z).wait_recv())

    first_y = (a_out, a_in, ya_s, ya_r)
    first_z = (b_out, b_in, za_s, za_r)
    back_z = (r_out, r_in, zb_s, zb_r)
    back_y = (t_out, t_in, yb_s, yb_r)
    for c in range(CHUNKS):
        y_start(*first_y, c)

    @pl.when(my_z != g)
    def _():
        remote(wpad, wsh, wz_s.at[0], wz_r.at[0], at_z((my_z + 1) % s.z)).wait_recv()

    def wy_slot(y):
        return wyin.at[y // s.yl, pl.ds(pl.multiple_of((y % s.yl) * ROWS16, ROWS16), ROWS16), :]

    others(s.y, my_y, lambda y: remote(wsh, wy_slot(my_y), wy_s.at[y], wy_r.at[my_y], at_y(y)).start())
    wyin[my_yh, pl.ds(pl.multiple_of(my_yl * ROWS16, ROWS16), ROWS16), :] = wsh[...]

    def first_turn(c):
        y_wait(*first_y, c)
        b_out[c] = mm(perm[...], a_in[c]).astype(BF16)
        z_start(*first_z, c)

    first_turn(0)

    others(s.y, my_y, lambda y: remote(wsh, wy_slot(y), wy_s.at[y], wy_r.at[y], at_y(y)).wait_recv())
    wide = s.yl * s.rows
    pick = one_hot(wide, table[3:4, : s.yl * ROWS16])

    def w_rows(yh, x, c):
        return weight.at[pl.ds(pl.multiple_of(grp_of(yh, x, c) * wide, wide), wide), :]

    for yh in range(s.yh):
        w_rows(yh, my_x, core)[...] = mm(pick, wyin[yh]).astype(BF16)

    def wx_copy(yh, x, slot):
        rows = w_rows(yh, slot, core)
        return remote(rows, rows, wx_s.at[x * s.yh + yh], wx_r.at[slot * s.yh + yh], at_x(x))

    def wc_copy(yh, x, c):
        rows = w_rows(yh, x, c)
        return remote(rows, rows, wc_s.at[x * s.yh + yh], wc_r.at[x * s.yh + yh], sibling)

    for yh in range(s.yh):
        others(s.x, my_x, lambda x, yh=yh: wx_copy(yh, x, my_x).start())
        wc_copy(yh, my_x, core).start()

    for c in range(1, CHUNKS):
        first_turn(c)

    feat[...] = one_hot(s.width, table[0:1, : s.width])
    ids = row_ids[...].astype(F32)
    down = lax.broadcasted_iota(jnp.int32, (s.slots, s.slots), 0)
    across = lax.broadcasted_iota(jnp.int32, (s.slots, s.slots), 1)
    id_col = jnp.sum(jnp.where(down == across, ids, 0.0), axis=1, keepdims=True)
    before = jnp.sum(jnp.where(ids < id_col, 1.0, 0.0), axis=1, keepdims=True)
    place = lax.broadcasted_iota(jnp.int32, (s.slots, 1), 0).astype(F32) - before
    limit = jnp.zeros((s.slots, 1), F32)
    for k in range(frames.shape[1]):
        limit = limit + jnp.where(id_col == k, frames[0:1, k : k + 1].astype(F32), 0.0)
    aud[...] = jnp.where(place >= limit, 1.0, 0.0)

    for x_step in range(1, s.x):
        x = (my_x + x_step) % s.x
        for yh in range(s.yh):
            wx_copy(yh, x, x).wait_recv()
            wc_copy(yh, x, core).start()

    for c in range(CHUNKS):
        z_wait(*first_z, c)
        packed[:, c * s.chunk : (c + 1) * s.chunk] = mm(rt[...], b_in[c], TN).astype(BF16)

    step_rows = 32

    def by_rows(body):
        def step(i, carry):
            body(pl.ds(pl.multiple_of(i * step_rows, step_rows), step_rows))
            return carry

        lax.fori_loop(0, s.slots // step_rows, step, 0)

    def norm(rows):
        values = packed[rows, :].astype(F32)
        centered = values - jnp.mean(values, axis=1, keepdims=True)
        variance = jnp.mean(centered * centered, axis=1, keepdims=True)
        inverse = lax.rsqrt(variance + EPSILON)
        unit = centered * inverse
        inv[rows, :] = inverse
        standard[rows, :] = unit
        audio = jnp.broadcast_to(aud[rows, :], unit.shape) > 0.5
        gain = jnp.where(audio, gains[1:2, :], gains[0:1, :])
        bias = jnp.where(audio, biases[1:2, :], biases[0:1, :])
        normed[rows, :] = (unit * gain + bias).astype(BF16)

    by_rows(norm)
    for h in range(2):
        normed_p[h] = mm(normed[...], feat[:, h * s.half : (h + 1) * s.half]).astype(BF16)

    def wc_all(body):
        for x in range(s.x):
            for yh in range(s.yh):
                body(wc_copy(yh, x, other))

    wc_all(lambda copy: copy.wait_recv())

    def project(i, carry):
        cols = pl.ds(pl.multiple_of(i * s.inner, LANES), s.inner)
        qkv[:, cols] = mm(normed[...], weight[:, cols]).astype(BF16)
        return carry

    lax.fori_loop(0, 3, project, 0)

    pair = 2 * HEAD_DIM
    scaling = 1.0 / HEAD_DIM**0.5

    def heads(i, carry):
        def part(k):
            return pl.ds(pl.multiple_of(k * s.inner + i * pair, LANES), pair)

        lane = lax.broadcasted_iota(jnp.int32, (1, pair), 1)
        masks = [jnp.where(lane < HEAD_DIM, 1.0, 0.0), jnp.where(lane < HEAD_DIM, 0.0, 1.0)]
        row_of = lax.broadcasted_iota(jnp.int32, (s.slots, s.slots), 0)
        col_of = lax.broadcasted_iota(jnp.int32, (s.slots, s.slots), 1)
        ids_row = row_ids[...].astype(F32)
        ids_col = jnp.sum(jnp.where(row_of == col_of, ids_row, 0.0), axis=1, keepdims=True)
        same = ids_row == ids_col
        q, k, v, do = qkv[:, part(0)], qkv[:, part(1)], qkv[:, part(2)], dout[:, part(0)]

        def split(a):
            return [a * m.astype(BF16) for m in masks]

        qs, ks, vs, dos = split(q), split(k), split(v), split(do)
        probs = []
        for a in range(2):
            scores = jnp.where(same, mm(qs[a], k, NT) * scaling, -1e30)
            exponent = jnp.exp(scores - jnp.max(scores, axis=1, keepdims=True))
            probs.append((exponent / jnp.sum(exponent, axis=1, keepdims=True)).astype(BF16))
        out = mm(jnp.concatenate(probs, axis=1), jnp.concatenate(vs, axis=0)).astype(BF16)
        attended[:, part(0)] = out
        delta = do.astype(F32) * out.astype(F32)
        grads = []
        for a in range(2):
            row_delta = jnp.sum(delta * masks[a], axis=1, keepdims=True)
            grad_probs = mm(dos[a], v, NT)
            grads.append((probs[a].astype(F32) * (grad_probs - row_delta) * scaling).astype(BF16))
        gqkv[:, part(0)] = mm(
            jnp.concatenate(grads, axis=1), jnp.concatenate(ks, axis=0)
        ).astype(BF16)
        gqkv[:, part(1)] = mm(
            jnp.concatenate(grads, axis=0), jnp.concatenate(qs, axis=0), TN
        ).astype(BF16)
        gqkv[:, part(2)] = mm(
            jnp.concatenate(probs, axis=0), jnp.concatenate(dos, axis=0), TN
        ).astype(BF16)
        return carry

    lax.fori_loop(0, s.inner // pair, heads, 0)

    def unproject(i, carry):
        rows = pl.ds(pl.multiple_of(i * s.chunk, s.chunk), s.chunk)
        gnorm[i] = mm(gqkv[...], weight[rows, :], NT)
        return carry

    lax.fori_loop(0, CHUNKS, unproject, 0)
    n_c[core] = jnp.zeros_like(n_c[0])

    def unnorm(rows):
        grad = jnp.concatenate([gnorm[c, rows, :] for c in range(CHUNKS)], axis=1)
        unit = standard[rows, :]
        audio = jnp.broadcast_to(aud[rows, :], unit.shape) > 0.5
        gain = jnp.where(audio, gains[1:2, :], gains[0:1, :])
        gain_term = grad * unit
        n_c[core] += jnp.concatenate(
            [
                jnp.sum(jnp.where(audio, 0.0, gain_term), axis=0, keepdims=True),
                jnp.sum(jnp.where(audio, gain_term, 0.0), axis=0, keepdims=True),
                jnp.sum(jnp.where(audio, 0.0, grad), axis=0, keepdims=True),
                jnp.sum(jnp.where(audio, grad, 0.0), axis=0, keepdims=True),
            ],
            axis=0,
        )
        scaled = grad * gain
        out = inv[rows, :] * (
            scaled
            - jnp.mean(scaled, axis=1, keepdims=True)
            - unit * jnp.mean(scaled * unit, axis=1, keepdims=True)
        )
        gpacked[rows, :] = out.astype(BF16)

    by_rows(unnorm)
    for c in range(CHUNKS):
        r_out[c] = mm(rt[...], gpacked[:, c * s.chunk : (c + 1) * s.chunk]).astype(BF16)
        z_start(*back_z, c)

    third = s.columns // 3

    def third_rows(k):
        return pl.ds(pl.multiple_of(k * third, third), third)

    def gc_copy(k):
        return remote(g_send.at[third_rows(k), :], g_in.at[third_rows(k), :], gc_s.at[k], gc_r.at[k], sibling)

    for k in range(3):
        g_send[third_rows(k), :] = mm(gqkv[:, k * third : (k + 1) * third], normed_p[other], TN).astype(BF16)
        gc_copy(k).start()

    def n_copy(buf, slot, peer, send, recv, device):
        return remote(buf.at[slot], buf.at[slot], send.at[peer], recv.at[slot], device)

    n_copy(n_c, core, other, nc_s, nc_r, sibling).start()

    for k in range(3):
        g_own[third_rows(k), :] = mm(gqkv[:, k * third : (k + 1) * third], normed_p[core], TN)

    def total(buf, count):
        result = buf[0]
        for k in range(1, count):
            result = result + buf[k]
        return result

    def n_start(buf, count, me, send, recv, at, value):
        buf[me] = value
        others(count, me, lambda p: n_copy(buf, me, p, send, recv, at(p)).start())

    def n_wait(buf, count, me, send, recv, at):
        others(count, me, lambda p: n_copy(buf, p, p, send, recv, at(p)).wait_recv())

    by_x = (n_x, s.x, my_x, nx_s, nx_r, at_x)
    by_y = (n_y, s.y, my_y, ny_s, ny_r, at_y)
    my_za, my_zb = my_z // s.zb, my_z % s.zb
    by_zb = (n_zb, s.zb, my_zb, nzb_s, nzb_r, lambda zb: at_z(my_za * s.zb + zb))
    by_za = (n_za, s.za, my_za, nza_s, nza_r, lambda za: at_z(za * s.zb + my_zb))

    n_copy(n_c, other, other, nc_s, nc_r, sibling).wait_recv()
    n_start(*by_x, total(n_c, s.c))

    def piece_rows(p):
        return pl.ds(pl.multiple_of(p * s.chip_block, ROWS16), s.chip_block)

    def gx_copy(yh, x, slot):
        return remote(
            x_out.at[piece_rows(yh * s.x + x), :], x_in.at[slot, yh],
            gx_s.at[x * s.yh + yh], gx_r.at[slot * s.yh + yh], at_x(x),
        )

    sent = 0
    for k in range(3):
        gc_copy(k).wait_recv()
        both = g_own[third_rows(k), :] + g_in[third_rows(k), :].astype(F32)
        g_own[third_rows(k), :] = both
        x_out[third_rows(k), :] = both.astype(BF16)
        while (sent + 1) * s.chip_block <= (k + 1) * third:
            yh, x = sent // s.x, sent % s.x

            @pl.when(x != my_x)
            def _(yh=yh, x=x):
                gx_copy(yh, x, my_x).start()

            sent += 1

    def back_turn(c):
        z_wait(*back_z, c)
        t_out[c] = mm(perm[...], r_in[c], TN).astype(BF16)
        y_start(*back_y, c)

    back_turn(0)
    n_wait(*by_x)
    n_start(*by_y, total(n_x, s.x))
    back_turn(1)

    spread = one_hot(s.half, table[1:2, : s.yl * LANES])
    for yh in range(s.yh):
        others(s.x, my_x, lambda x, yh=yh: gx_copy(yh, x, x).wait_recv())
        piece = g_own[piece_rows(yh * s.x + my_x), :]
        for step in range(1, s.x):
            piece = piece + x_in[(my_x + step) % s.x, yh].astype(F32)
        wide_piece = mm(piece.astype(BF16), spread).astype(BF16)
        for yl in range(s.yl):
            y_out[yh * s.yl + yl] = wide_piece[:, yl * LANES : (yl + 1) * LANES]
    others(s.y, my_y, lambda y: remote(y_out.at[y], y_in.at[my_y], gy_s.at[y], gy_r.at[my_y], at_y(y)).start())
    y_in[my_y] = y_out[my_y]

    n_wait(*by_y)
    n_start(*by_zb, total(n_y, s.y))
    back_turn(2)

    others(s.y, my_y, lambda y: remote(y_out.at[y], y_in.at[y], gy_s.at[y], gy_r.at[y], at_y(y)).wait_recv())
    piece = y_in[0].astype(F32)
    for y in range(1, s.y):
        piece = piece + y_in[y].astype(F32)
    apart = one_hot(s.z * ROWS8, table[4:5, :LANES])
    z_out[...] = mm(apart, piece.astype(BF16), NT)

    def z_tile(z):
        return z_out.at[pl.ds(pl.multiple_of(z * ROWS8, ROWS8), ROWS8), :]

    others(s.z, my_z, lambda z: remote(z_tile(z), z_in.at[my_z], gz_s.at[z], gz_r.at[my_z], at_z(z)).start())
    z_in[my_z] = z_out[pl.ds(pl.multiple_of(my_z * ROWS8, ROWS8), ROWS8), :]

    n_wait(*by_zb)
    n_start(*by_za, total(n_zb, s.zb))

    def home(c):
        y_wait(*back_y, c)
        grad_tokens[:, c * s.chunk : (c + 1) * s.chunk] = mm(pt[...], t_in[c]).astype(BF16)

    home(0)
    home(1)
    others(s.z, my_z, lambda z: remote(z_tile(z), z_in.at[z], gz_s.at[z], gz_r.at[z], at_z(z)).wait_recv())
    own = total(z_in, s.z)
    f_send[...] = own
    f_copy = remote(f_send, f_in, gf_s.at[0], gf_r.at[0], sibling)
    f_copy.start()
    home(2)
    n_wait(*by_za)
    norms = total(n_za, s.za)
    grad_scale[...] = norms[0:2]
    grad_shift[...] = norms[2:4]
    f_copy.wait_recv()
    first = core == 0
    theirs = f_in[...]
    low, high = jnp.where(first, own, theirs), jnp.where(first, theirs, own)
    for part, (at, value) in enumerate(((0, low), (s.half_rows, high))):
        mine = jnp.where(first, value[:, : s.col_block], value[:, s.col_block :])
        grad_weight[at : at + s.half_rows, :] = mine[: s.half_rows]

    @pl.when(my_z == g)
    def _():
        others(s.z, my_z, lambda z: remote(wpad, wsh, wz_s.at[z], wz_r.at[0], at_z(z)).wait_send())

    for c in range(CHUNKS):
        for way in (first_y, back_y):
            others(s.yl, my_yl, lambda y: y_copy(*way, c, y, my_yl).wait_send())
        for way in (first_z, back_z):
            others(s.z, my_z, lambda z: z_copy(*way, c, z, my_z).wait_send())
    others(s.y, my_y, lambda y: remote(wsh, wy_slot(my_y), wy_s.at[y], wy_r.at[my_y], at_y(y)).wait_send())
    for yh in range(s.yh):
        others(s.x, my_x, lambda x, yh=yh: wx_copy(yh, x, my_x).wait_send())
        others(s.x, my_x, lambda x, yh=yh: gx_copy(yh, x, my_x).wait_send())
    wc_all(lambda copy: copy.wait_send())
    for k in range(3):
        gc_copy(k).wait_send()
    others(s.y, my_y, lambda y: remote(y_out.at[y], y_in.at[my_y], gy_s.at[y], gy_r.at[my_y], at_y(y)).wait_send())
    others(s.z, my_z, lambda z: remote(z_tile(z), z_in.at[my_z], gz_s.at[z], gz_r.at[my_z], at_z(z)).wait_send())
    f_copy.wait_send()
    n_copy(n_c, core, other, nc_s, nc_r, sibling).wait_send()
    for buf, count, me, send, recv, at in (by_x, by_y, by_zb, by_za):
        others(count, me, lambda p: n_copy(buf, me, p, send, recv, at(p)).wait_send())


def shards(
    tokens, send_order, recv_order, row_ids, frames, norm_scale, norm_shift, qkv_weight, d_out
):
    slots, width = tokens.shape
    columns = qkv_weight.shape[1]
    s = Sizes(lax.axis_size("grp"), lax.axis_size("fsdp"), slots, width, columns)
    whole = pl.BlockSpec(memory_space=pltpu.VMEM)
    vm, dma = pltpu.VMEM, pltpu.SemaphoreType.DMA
    moved = vm((CHUNKS, slots, s.chunk), BF16)
    norms = (4, width)
    scratch = [
        vm((slots, slots), BF16), vm((slots, slots), BF16), vm((slots, slots), BF16),
        vm((width, width), BF16), moved, moved, moved, moved, vm((slots, width), BF16),
        vm((ROWS16, columns), BF16), vm((ROWS16, columns), BF16),
        vm((s.yh, s.yl * ROWS16, columns), BF16), vm((width, columns), BF16),
        vm((slots, 1), F32), vm((slots, width), F32), vm((slots, 1), F32),
        vm((slots, width), BF16), vm((2, slots, s.half), BF16),
        vm((slots, columns), BF16), vm((slots, columns), BF16),
        vm((CHUNKS, slots, s.chunk), F32), vm((slots, width), BF16),
        moved, moved, moved, moved,
        vm((columns, s.half), BF16), vm((columns, s.half), F32), vm((columns, s.half), BF16),
        vm((columns, s.half), BF16), vm((s.x, s.yh, s.chip_block, s.half), BF16),
        vm((s.y, s.chip_block, LANES), BF16), vm((s.y, s.chip_block, LANES), BF16),
        vm((s.z * ROWS8, s.chip_block), F32), vm((s.z, ROWS8, s.chip_block), F32),
        vm((ROWS8, s.chip_block), F32), vm((ROWS8, s.chip_block), F32),
        vm((s.c,) + norms, F32), vm((s.x,) + norms, F32), vm((s.y,) + norms, F32),
        vm((s.zb,) + norms, F32), vm((s.za,) + norms, F32),
    ]
    y3, z3 = CHUNKS * s.yl, CHUNKS * s.z
    xy = s.x * s.yh
    counts = [y3, y3, z3, z3, y3, y3, z3, z3]
    counts += [s.z, 1, s.y, s.y, xy, xy, xy, xy]
    counts += [3, 3, xy, xy, s.y, s.y, s.z, s.z, 1, 1]
    counts += [s.c, s.c, s.x, s.x, s.y, s.y, s.zb, s.zb, s.za, s.za]
    scratch += [dma((n,)) for n in counts]
    sds = jax.ShapeDtypeStruct
    return pl.pallas_call(
        functools.partial(kernel, s),
        out_shape=(
            sds((slots, s.inner), BF16), sds((slots, width), BF16),
            sds((s.rows, s.col_block), F32), sds((2, width), F32), sds((2, width), F32),
        ),
        in_specs=[whole] * 10,
        out_specs=(whole,) * 5,
        scratch_shapes=scratch,
        compiler_params=pltpu.CompilerParams(
            collective_id=0, has_side_effects=True, vmem_limit_bytes=56 * 1024 * 1024
        ),
        cost_estimate=pl.CostEstimate(
            flops=2_000_000_000, bytes_accessed=3_000_000, transcendentals=400_000
        ),
        name="joint_block",
    )(
        tokens, send_order, recv_order, row_ids, frames, norm_scale, norm_shift, qkv_weight, d_out,
        jnp.asarray(index_rows(s)),
    )


def solution(mesh):
    rows = P(("grp", "fsdp"), None)
    return jax.shard_map(
        shards,
        mesh=mesh,
        in_specs=(rows, rows, rows, rows, rows, P(), P(), P("fsdp", None), rows),
        out_specs=(rows, rows, P("fsdp", "grp"), P(), P()),
        check_vma=False,
    )
```

```python
import functools

import jax
import jax.numpy as jnp
import numpy as np
from jax import lax
from jax.experimental import pallas as pl
from jax.experimental.pallas import tpu as pltpu
from jax.sharding import PartitionSpec as P

HEAD_DIM = 64
EPSILON = 1e-06
MESH = pl.DeviceIdType.MESH
BF16 = jnp.bfloat16
F32 = jnp.float32
ROWS16 = 16
ROWS8 = 8
LANES = 128
CHUNKS = 3
NORM_ROWS = 64
UNNORM_ROWS = 64


class Sizes:
    def __init__(self, grp, fsdp, slots, width, columns):
        self.yh, self.x, self.c = {16: (2, 4, 2), 4: (1, 2, 2), 8: (2, 2, 2)}[grp]
        self.yl = 4 if fsdp == 64 else 2
        self.z = fsdp // self.yl
        self.zb = 4 if self.z == 16 else 2
        self.za = self.z // self.zb
        self.y = self.yh * self.yl
        self.slots, self.width, self.columns = slots, width, columns
        self.inner = columns // 3
        self.per_peer = slots // fsdp
        self.rows = width // fsdp
        self.half_rows = self.rows // 2
        self.col_block = columns // grp
        self.chip_block = self.col_block * self.c
        self.pieces = self.yh * self.x
        self.chunk = width // CHUNKS
        self.half = width // 2
        self.z_lanes = self.z * self.half_rows
        self.fold = (columns // LANES * 2 // 9) * LANES
        self.kept = columns - self.fold


def index_rows(s):
    table = np.full((8, max(s.width, s.yl * LANES, s.slots)), -1, np.int32)
    for j in range(s.width):
        h, r = divmod(j, s.half)
        yl, r = divmod(r, s.z_lanes)
        z, i = divmod(r, s.half_rows)
        table[0, j] = (z * s.yl + yl) * s.rows + h * s.half_rows + i
    for yl in range(s.yl):
        for j in range(s.z_lanes):
            table[1, yl * LANES + j] = yl * s.z_lanes + j
    for yl in range(s.yl):
        for z in range(s.z):
            for r in range(s.per_peer):
                q = (yl * s.z + z) * s.per_peer + r
                table[2, q] = (z * s.yl + yl) * s.per_peer + r
    for yl in range(s.yl):
        for i in range(s.rows):
            table[3, yl * ROWS16 + i] = yl * s.rows + i
            table[5 + i % 3, yl * ROWS16 + s.rows + i // 3] = yl * s.rows + i
    for z in range(s.z):
        for i in range(s.half_rows):
            table[4, z * s.half_rows + i] = z * ROWS8 + i
    return table


def one_hot(count, row):
    ids = lax.broadcasted_iota(jnp.int32, (count, row.shape[1]), 0)
    return jnp.where(ids == row, 1.0, 0.0).astype(BF16)


def mm(a, b, dims=((1,), (0,))):
    return lax.dot_general(a, b, (dims, ((), ())), preferred_element_type=F32)


TN = ((0,), (0,))
NT = ((1,), (1,))


def kernel(
    s, tok_h, send_order_h, recv_order_h, row_ids_h, frames_h, gains_h, biases_h, wshard_h, dout_h, table_h,
    attended_h, grad_tokens_h, grad_weight_h, grad_scale_h, grad_shift_h,
    tok, send_order, recv_order, row_ids, frames, gains, biases, wshard, dout, table,
    attended, grad_tokens, grad_weight, grad_scale, grad_shift,
    pt, pt_q, perm, rt, rt_q, feat, a_out, a_in, b_out, b_in, packed, wpad, wsh, wyin, weight,
    aud, same, standard, inv, normed, normed_p, qkv, gqkv, gnorm, gpacked,
    r_out, r_in, t_out, t_in, g_send, g_own, g_in, x_out, x_in, y_out, y_in, z_out, z_in,
    f_send, f_in, n_c, n_x, n_y, n_zb, n_za,
    load, store,
    ya_s, ya_r, za_s, za_r, yb_s, yb_r, zb_s, zb_r,
    wz_s, wz_r, wy_s, wy_r, wx_s, wx_r, wc_s, wc_r,
    gc_s, gc_r, gx_s, gx_r, gy_s, gy_r, gz_s, gz_r, gf_s, gf_r,
    nc_s, nc_r, nx_s, nx_r, ny_s, ny_r, nzb_s, nzb_r, nza_s, nza_r,
):
    g = lax.axis_index("grp")
    f = lax.axis_index("fsdp")
    core = g % s.c
    my_x = (g // s.c) % s.x
    my_yh = g // (s.c * s.x)
    my_z = f // s.yl
    my_yl = f % s.yl
    my_y = my_yh * s.yl + my_yl
    other = 1 - core

    def grp_of(yh, x, c):
        return (yh * s.x + x) * s.c + c

    def at_z(z):
        return (g, z * s.yl + my_yl)

    def at_yl(yl):
        return (g, my_z * s.yl + yl)

    def at_y(y):
        return (grp_of(y // s.yl, my_x, core), my_z * s.yl + y % s.yl)

    def at_x(x):
        return (grp_of(my_yh, x, core), f)

    sibling = (grp_of(my_yh, my_x, other), f)

    def others(count, me, body):
        def step(i, carry):
            body((me + count // 2 + (i + 1) // 2 * (1 - 2 * (i % 2))) % count)
            return carry

        lax.fori_loop(0, count - 1, step, 0)

    def remote(src, dst, send, recv, device):
        return pltpu.make_async_remote_copy(
            src_ref=src, dst_ref=dst, send_sem=send, recv_sem=recv,
            device_id=device, device_id_type=MESH,
        )

    ends = []

    def rows_of(ref, k, count):
        return ref.at[pl.ds(pl.multiple_of(k * count, count), count), :]

    class Exchange:
        def __init__(self, src, dst, rows, count, me, send, recv, at, spread=True):
            self.src, self.dst, self.rows, self.count, self.me = src, dst, rows, count, me
            self.send, self.recv, self.at, self.spread = send, recv, at, spread

        def copy(self, p):
            block = rows_of(self.src, p if self.spread else 0, self.rows)
            return remote(block, rows_of(self.dst, self.me, self.rows), self.send, self.recv, self.at(p))

        def start(self):
            others(self.count, self.me, lambda p: self.copy(p).start())
            self.started()

        def start_one(self, p):
            @pl.when(p != self.me)
            def _():
                self.copy(p).start()

        def started(self):
            ends.append(self.whole().wait_send)
            mine = rows_of(self.src, self.me if self.spread else 0, self.rows)
            rows_of(self.dst, self.me, self.rows)[...] = mine[...]

        def whole(self):
            part = self.dst.at[pl.ds(0, (self.count - 1) * self.rows), :]
            return remote(part, part, self.send, self.recv, self.at((self.me + 1) % self.count))

        def wait(self):
            self.whole().wait_recv()

    barrier = pltpu.get_barrier_semaphore()

    def greet(device):
        pl.semaphore_signal(barrier, inc=1, device_id=device, device_id_type=MESH)

    others(s.z, my_z, lambda z: greet(at_z(z)))
    others(s.y, my_y, lambda y: greet(at_y(y)))
    others(s.x, my_x, lambda x: greet(at_x(x)))
    greet(sibling)

    inputs = [
        (send_order_h, send_order), (table_h, table), (tok_h, tok), (wshard_h, wshard), (recv_order_h, recv_order),
        (row_ids_h, row_ids), (frames_h, frames), (gains_h, gains), (biases_h, biases), (dout_h, dout),
    ]
    loads = [pltpu.make_async_copy(src, dst, load.at[i]) for i, (src, dst) in enumerate(inputs)]
    for copy in loads:
        copy.start()

    for copy in loads:
        copy.wait()
    to_q = one_hot(s.slots, table[2:3, : s.slots])
    perm[...] = to_q
    pt[...] = one_hot(s.slots, send_order[...])
    pt_q[...] = mm(pt[...], to_q).astype(BF16)
    rt[...] = one_hot(s.slots, recv_order[...])
    rt_q[...] = mm(to_q, rt[...], TN).astype(BF16)
    wpad[...] = jnp.zeros_like(wpad)
    wpad[0 : s.rows, :] = wshard[:, : s.kept]
    for k in range(3 if s.fold else 0):
        down_rows = one_hot(s.rows, table[5 + k : 6 + k, :ROWS16])
        folded = mm(down_rows, wshard[:, s.kept :], TN).astype(BF16)
        wpad[:, k * s.fold : (k + 1) * s.fold] += folded
    for c in range(CHUNKS):
        a_out[c] = mm(pt_q[...], tok[:, c * s.chunk : (c + 1) * s.chunk], TN).astype(BF16)
    pl.semaphore_wait(barrier, (s.z - 1) + (s.y - 1) + (s.x - 1) + 1)

    run = s.slots // s.yl
    block = s.slots // s.z

    def along_yl(out, into, send, recv):
        return [
            Exchange(out.at[c], into.at[c], run, s.yl, my_yl, send.at[c], recv.at[c], at_yl) for c in range(CHUNKS)
        ]

    def along_z(out, into, send, recv):
        return [
            Exchange(out.at[c], into.at[c], block, s.z, my_z, send.at[c], recv.at[c], at_z) for c in range(CHUNKS)
        ]

    first_y = along_yl(a_out, a_in, ya_s, ya_r)
    first_z = along_z(b_out, b_in, za_s, za_r)
    back_y = along_yl(r_out, r_in, yb_s, yb_r)
    back_z = along_z(t_out, t_in, zb_s, zb_r)

    def wz_copy(z):
        return remote(wpad, wsh, wz_s.at[0], wz_r.at[0], at_z(z))

    @pl.when(my_z == g)
    def _():
        others(s.z, my_z, lambda z: wz_copy(z).start())
        wsh[...] = wpad[...]

    first_y[0].start()
    first_y[1].start()

    def first_turn(c):
        first_y[c].wait()
        if c == 0:
            for later in first_y[2:]:
                later.start()
        b_out[c] = mm(perm[...], a_in[c]).astype(BF16)
        first_z[c].start()

    feat[...] = one_hot(s.width, table[0:1, : s.width])
    ids = row_ids[...].astype(F32)
    down = lax.broadcasted_iota(jnp.int32, (s.slots, s.slots), 0)
    across = lax.broadcasted_iota(jnp.int32, (s.slots, s.slots), 1)
    id_col = jnp.sum(jnp.where(down == across, ids, 0.0), axis=1, keepdims=True)
    before = jnp.sum(jnp.where(ids < id_col, 1.0, 0.0), axis=1, keepdims=True)
    place = lax.broadcasted_iota(jnp.int32, (s.slots, 1), 0).astype(F32) - before
    limit = jnp.zeros((s.slots, 1), F32)
    for k in range(frames.shape[1]):
        limit = limit + jnp.where(id_col == k, frames[0:1, k : k + 1].astype(F32), 0.0)
    aud[...] = jnp.where(place >= limit, 1.0, 0.0)
    same[...] = jnp.where(ids == id_col, 1.0, 0.0)

    wide = s.yl * s.rows
    pick = one_hot(wide, table[3:4, : s.yl * ROWS16])

    def w_rows(yh, x, c):
        return rows_of(weight, grp_of(yh, x, c), wide)

    def wx_copy(yh, x, slot):
        rows = w_rows(yh, slot, core)
        return remote(rows, rows, wx_s.at[x * s.yh + yh], wx_r.at[slot * s.yh + yh], at_x(x))

    def wc_copy(yh, x, c):
        rows = w_rows(yh, x, c)
        return remote(rows, rows, wc_s.at[x * s.yh + yh], wc_r.at[x * s.yh + yh], sibling)

    first_turn(0)

    @pl.when(my_z != g)
    def _():
        wz_copy((my_z + 1) % s.z).wait_recv()

    def wy_copy(y):
        slot = rows_of(wyin, my_y, ROWS16)
        return remote(wsh, slot, wy_s.at[0], wy_r.at[my_yh], at_y(y))

    def wy_part(at, count, send, recv):
        part = wyin.at[pl.ds(at, count * ROWS16), :]
        return remote(part, part, send, recv, at_y((my_y + 1) % s.y))

    others(s.y, my_y, lambda y: wy_copy(y).start())
    ends.append(wy_part(0, s.y - 1, wy_s.at[0], wy_r.at[0]).wait_send)
    rows_of(wyin, my_y, ROWS16)[...] = wsh[...]
    first_turn(1)
    first_turn(2)

    run16 = s.yl * ROWS16
    for step in range(s.yh):
        yh = (my_yh + step) % s.yh
        wy_part(0, s.yl - 1 if step == 0 else s.yl, wy_s.at[0], wy_r.at[yh]).wait_recv()
        shards_of = wyin[pl.ds(pl.multiple_of(yh * run16, run16), run16), :]
        w_block = w_rows(yh, my_x, core)
        w_block[:, 0 : s.kept] = mm(pick, shards_of).astype(BF16)
        if s.fold:
            w_block[:, s.kept :] = sum(
                mm(one_hot(wide, table[5 + k : 6 + k, : s.yl * ROWS16]), shards_of[:, k * s.fold : (k + 1) * s.fold])
                for k in range(3)
            ).astype(BF16)
        others(s.x, my_x, lambda x, yh=yh: wx_copy(yh, x, my_x).start())
        wc_copy(yh, my_x, core).start()

    def unpack(c):
        first_z[c].wait()
        packed[:, c * s.chunk : (c + 1) * s.chunk] = mm(rt[...], b_in[c], TN).astype(BF16)

    def pass_on(step):
        yh = (my_yh + step) % s.yh

        def one(x):
            wx_copy(yh, x, x).wait_recv()
            wc_copy(yh, x, core).start()

        others(s.x, my_x, one)

    for c in range(CHUNKS - 1):
        unpack(c)
    for step in range(s.yh - 1):
        pass_on(step)
    unpack(CHUNKS - 1)

    def by_rows(step_rows, body):
        def step(i, carry):
            body(pl.ds(pl.multiple_of(i * step_rows, step_rows), step_rows))
            return carry

        lax.fori_loop(0, s.slots // step_rows, step, 0)

    def norm(rows):
        values = packed[rows, :].astype(F32)
        centered = values - jnp.mean(values, axis=1, keepdims=True)
        variance = jnp.mean(centered * centered, axis=1, keepdims=True)
        inverse = lax.rsqrt(variance + EPSILON)
        unit = centered * inverse
        inv[rows, :] = inverse
        standard[rows, :] = unit
        audio = jnp.broadcast_to(aud[rows, :], unit.shape) > 0.5
        gain = jnp.where(audio, gains[1:2, :], gains[0:1, :])
        bias = jnp.where(audio, biases[1:2, :], biases[0:1, :])
        normed[rows, :] = (unit * gain + bias).astype(BF16)

    by_rows(NORM_ROWS, norm)
    pass_on(s.yh - 1)
    for h in range(2):
        normed_p[h] = mm(normed[...], feat[:, h * s.half : (h + 1) * s.half]).astype(BF16)

    def wc_all(body):
        for x in range(s.x):
            for yh in range(s.yh):
                body(wc_copy(yh, x, other))

    wc_all(lambda copy: copy.wait_recv())

    def project(i, carry):
        cols = pl.ds(pl.multiple_of(i * s.inner, LANES), s.inner)
        qkv[:, cols] = mm(normed[...], weight[:, cols]).astype(BF16)
        return carry

    lax.fori_loop(0, 3, project, 0, unroll=True)

    pair = 2 * HEAD_DIM
    scaling = 1.0 / HEAD_DIM**0.5

    def heads(i, carry):
        def part(k):
            return pl.ds(pl.multiple_of(k * s.inner + i * pair, LANES), pair)

        lane = lax.broadcasted_iota(jnp.int32, (1, pair), 1)
        masks = [jnp.where(lane < HEAD_DIM, 1.0, 0.0), jnp.where(lane < HEAD_DIM, 0.0, 1.0)]
        q, k, v, do = qkv[:, part(0)], qkv[:, part(1)], qkv[:, part(2)], dout[:, part(0)]

        def split(a):
            return [a * m.astype(BF16) for m in masks]

        qs, ks, vs, dos = split(q), split(k), split(v), split(do)
        probs = []
        for a in range(2):
            scores = jnp.where(same[...] > 0.5, mm(qs[a], k, NT) * scaling, -1e30)
            exponent = jnp.exp(scores - jnp.max(scores, axis=1, keepdims=True))
            probs.append((exponent / jnp.sum(exponent, axis=1, keepdims=True)).astype(BF16))
        out = mm(jnp.concatenate(probs, axis=1), jnp.concatenate(vs, axis=0)).astype(BF16)
        attended[:, part(0)] = out
        delta = do.astype(F32) * out.astype(F32)
        grads = []
        for a in range(2):
            row_delta = jnp.sum(delta * masks[a], axis=1, keepdims=True)
            grad_probs = mm(dos[a], v, NT)
            grads.append((probs[a].astype(F32) * (grad_probs - row_delta) * scaling).astype(BF16))
        gqkv[:, part(0)] = mm(
            jnp.concatenate(grads, axis=1), jnp.concatenate(ks, axis=0)
        ).astype(BF16)
        gqkv[:, part(1)] = mm(
            jnp.concatenate(grads, axis=0), jnp.concatenate(qs, axis=0), TN
        ).astype(BF16)
        gqkv[:, part(2)] = mm(
            jnp.concatenate(probs, axis=0), jnp.concatenate(dos, axis=0), TN
        ).astype(BF16)
        return carry

    lax.fori_loop(0, s.inner // pair, heads, 0, unroll=True)
    stores = []

    def keep(src, dst):
        copy = pltpu.make_async_copy(src, dst, store.at[len(stores)])
        copy.start()
        stores.append(copy)

    keep(attended, attended_h)

    third = s.columns // 3

    def third_rows(k):
        return pl.ds(k * third, third)

    def gc_copy(k):
        return remote(g_send.at[third_rows(k), :], g_in.at[third_rows(k), :], gc_s.at[k], gc_r.at[k], sibling)

    for k in range(3):
        g_send[third_rows(k), :] = mm(gqkv[:, k * third : (k + 1) * third], normed_p[other], TN).astype(BF16)
        gc_copy(k).start()
        ends.append(gc_copy(k).wait_send)

    def unproject(i, carry):
        rows = pl.ds(pl.multiple_of(i * s.chunk, s.chunk), s.chunk)
        gnorm[i] = mm(gqkv[...], weight[rows, :], NT)
        return carry

    lax.fori_loop(0, CHUNKS, unproject, 0, unroll=True)
    def piece_rows(p):
        return pl.ds(pl.multiple_of(p * s.chip_block, ROWS16), s.chip_block)

    def gx_copy(yh, x, slot):
        return remote(x_out.at[piece_rows(yh * s.x + x), :], x_in.at[yh, slot], gx_s.at[yh], gx_r.at[yh], at_x(x))

    sent = 0
    for k in range(3):
        g_own[third_rows(k), :] = mm(gqkv[:, k * third : (k + 1) * third], normed_p[core], TN)
        gc_copy(k).wait_recv()
        both = g_own[third_rows(k), :] + g_in[third_rows(k), :].astype(F32)
        g_own[third_rows(k), :] = both
        x_out[third_rows(k), :] = both.astype(BF16)
        while (sent + 1) * s.chip_block <= (k + 1) * third:
            yh, x = sent // s.x, sent % s.x

            @pl.when(x != my_x)
            def _(yh=yh, x=x):
                gx_copy(yh, x, my_x).start()

            sent += 1
    gx_all = []
    for yh in range(s.yh):
        part = x_in.at[yh, pl.ds(0, s.x - 1)]
        gx_all.append(remote(part, part, gx_s.at[yh], gx_r.at[yh], at_x((my_x + 1) % s.x)))
        ends.append(gx_all[yh].wait_send)

    my_za, my_zb = my_z // s.zb, my_z % s.zb
    n_zb[my_zb] = jnp.zeros_like(n_zb[0])

    def unnorm(rows):
        grad = jnp.concatenate([gnorm[c, rows, :] for c in range(CHUNKS)], axis=1)
        unit = standard[rows, :]
        audio = jnp.broadcast_to(aud[rows, :], unit.shape) > 0.5
        gain = jnp.where(audio, gains[1:2, :], gains[0:1, :])
        gain_term = grad * unit
        n_zb[my_zb] += jnp.concatenate(
            [
                jnp.sum(jnp.where(audio, 0.0, gain_term), axis=0, keepdims=True),
                jnp.sum(jnp.where(audio, gain_term, 0.0), axis=0, keepdims=True),
                jnp.sum(jnp.where(audio, 0.0, grad), axis=0, keepdims=True),
                jnp.sum(jnp.where(audio, grad, 0.0), axis=0, keepdims=True),
            ],
            axis=0,
        )
        scaled = grad * gain
        out = inv[rows, :] * (
            scaled
            - jnp.mean(scaled, axis=1, keepdims=True)
            - unit * jnp.mean(scaled * unit, axis=1, keepdims=True)
        )
        gpacked[rows, :] = out.astype(BF16)

    by_rows(UNNORM_ROWS, unnorm)

    def total(buf, count):
        result = buf[0]
        for k in range(1, count):
            result = result + buf[k]
        return result

    class Sum:
        def __init__(self, buf, count, me, send, recv, at):
            self.buf, self.count, self.me, self.at = buf, count, me, at
            self.send, self.recv = send.at[0], recv.at[0]

        def start(self, value=None):
            if value is not None:
                self.buf[self.me] = value
            mine = self.buf.at[self.me]
            others(self.count, self.me, lambda p: remote(mine, mine, self.send, self.recv, self.at(p)).start())
            ends.append(self.whole().wait_send)

        def whole(self):
            part = self.buf.at[pl.ds(0, self.count - 1)]
            return remote(part, part, self.send, self.recv, self.at((self.me + 1) % self.count))

        def result(self):
            self.whole().wait_recv()
            return total(self.buf, self.count)

    sum_zb = Sum(n_zb, s.zb, my_zb, nzb_s, nzb_r, lambda zb: at_z(my_za * s.zb + zb))
    sum_za = Sum(n_za, s.za, my_za, nza_s, nza_r, lambda za: at_z(za * s.zb + my_zb))
    sum_c = Sum(n_c, s.c, core, nc_s, nc_r, lambda c: (grp_of(my_yh, my_x, c), f))
    sum_y = Sum(n_y, s.y, my_y, ny_s, ny_r, at_y)
    sum_x = Sum(n_x, s.x, my_x, nx_s, nx_r, at_x)
    sum_zb.start()

    for c in range(CHUNKS):
        r_out[c] = mm(rt_q[...], gpacked[:, c * s.chunk : (c + 1) * s.chunk]).astype(BF16)
        back_y[c].start()

    def back_turn(c):
        back_y[c].wait()
        t_out[c] = mm(perm[...], r_in[c]).astype(BF16)
        back_z[c].start()

    sum_za.start(sum_zb.result())
    back_turn(0)

    spread = one_hot(s.half, table[1:2, : s.yl * LANES])
    gy = Exchange(y_out, y_in, s.chip_block, s.y, my_y, gy_s.at[0], gy_r.at[0], at_y)
    for yh in range(s.yh):
        gx_all[yh].wait_recv()
        piece = g_own[piece_rows(yh * s.x + my_x), :]
        for step in range(1, s.x):
            piece = piece + x_in[yh, (my_x + step) % s.x].astype(F32)
        wide_piece = mm(piece.astype(BF16), spread).astype(BF16)
        for yl in range(s.yl):
            at = (yh * s.yl + yl) * s.chip_block
            y_out[at : at + s.chip_block, :] = wide_piece[:, yl * LANES : (yl + 1) * LANES]
            gy.start_one(yh * s.yl + yl)
        if yh == 0:
            back_turn(1)
    gy.started()
    back_turn(2)
    sum_c.start(sum_za.result())
    sum_y.start(sum_c.result())

    gy.wait()
    piece = y_in[0 : s.chip_block, :].astype(F32)
    for y in range(1, s.y):
        piece = piece + y_in[y * s.chip_block : (y + 1) * s.chip_block, :].astype(F32)
    apart = one_hot(s.z * ROWS8, table[4:5, :LANES])
    z_out[...] = mm(apart, piece.astype(BF16), NT)
    gz = Exchange(z_out, z_in, ROWS8, s.z, my_z, gz_s.at[0], gz_r.at[0], at_z)
    gz.start()
    sum_x.start(sum_y.result())

    def home(c):
        back_z[c].wait()
        grad_tokens[c] = mm(pt[...], t_in[c]).astype(BF16)
        keep(grad_tokens.at[c], grad_tokens_h.at[:, pl.ds(c * s.chunk, s.chunk)])

    home(0)
    home(1)

    @pl.when(my_z == g)
    def _():
        part = weight.at[pl.ds(0, (s.z - 1) * ROWS16), pl.ds(0, s.kept)]
        remote(part, part, wz_s.at[0], wz_r.at[0], at_z((my_z + 1) % s.z)).wait_send()

    others(s.x, my_x, lambda x: [wx_copy(yh, x, my_x).wait_send() for yh in range(s.yh)])
    wc_all(lambda copy: copy.wait_send())
    for wait in ends[:-2]:
        wait()
    last_ends = ends[-2:]
    del ends[:]
    gz.wait()
    own = z_in[0:ROWS8, :]
    for z in range(1, s.z):
        own = own + z_in[z * ROWS8 : (z + 1) * ROWS8, :]
    f_send[...] = own
    f_copy = remote(f_send, f_in, gf_s.at[0], gf_r.at[0], sibling)
    f_copy.start()
    ends.append(f_copy.wait_send)
    home(2)
    norms = sum_x.result()
    grad_scale[...] = norms[0:2]
    grad_shift[...] = norms[2:4]
    keep(grad_scale, grad_scale_h)
    keep(grad_shift, grad_shift_h)
    f_copy.wait_recv()
    first = core == 0
    theirs = f_in[...]
    low, high = jnp.where(first, own, theirs), jnp.where(first, theirs, own)
    for at, value in ((0, low), (s.half_rows, high)):
        mine = jnp.where(first, value[:, : s.col_block], value[:, s.col_block :])
        grad_weight[at : at + s.half_rows, :] = mine[: s.half_rows]
    keep(grad_weight, grad_weight_h)

    for wait in last_ends + ends:
        wait()
    for copy in stores:
        copy.wait()


def copy_out(*refs):
    count = (len(refs) - 2) // 3
    sources, targets, held = refs[:count], refs[count : 2 * count], refs[2 * count : 3 * count]
    load, store = refs[3 * count :]
    loads = [pltpu.make_async_copy(sources[i], held[i], load.at[i]) for i in range(count)]
    stores = [pltpu.make_async_copy(held[i], targets[i], store.at[i]) for i in range(count)]
    for copy in loads:
        copy.start()
    for i in range(count):
        loads[i].wait()
        stores[i].start()
    for copy in stores:
        copy.wait()


def shards(
    tokens, send_order, recv_order, row_ids, frames, norm_scale, norm_shift, qkv_weight, d_out
):
    slots, width = tokens.shape
    columns = qkv_weight.shape[1]
    s = Sizes(lax.axis_size("grp"), lax.axis_size("fsdp"), slots, width, columns)
    whole = pl.BlockSpec(memory_space=pl.ANY)
    vm, dma = pltpu.VMEM, pltpu.SemaphoreType.DMA
    moved = vm((CHUNKS, slots, s.chunk), BF16)
    norms = (4, width)
    args = (
        tokens, send_order, recv_order, row_ids, frames, norm_scale, norm_shift, qkv_weight, d_out,
        jnp.asarray(index_rows(s)),
    )
    sds = jax.ShapeDtypeStruct
    outs = (
        sds((slots, s.inner), BF16), sds((slots, width), BF16),
        sds((s.rows, s.col_block), F32), sds((2, width), F32), sds((2, width), F32),
    )
    scratch = [vm(a.shape, a.dtype) for a in args]
    scratch += [vm((slots, s.inner), BF16), moved]
    scratch += [vm(a.shape, a.dtype) for a in outs[2:]]
    scratch += [
        vm((slots, slots), BF16), vm((slots, slots), BF16), vm((slots, slots), BF16),
        vm((slots, slots), BF16), vm((slots, slots), BF16),
        vm((width, width), BF16), moved, moved, moved, moved, vm((slots, width), BF16),
        vm((ROWS16, s.kept), BF16), vm((ROWS16, s.kept), BF16),
        vm((s.y * ROWS16, s.kept), BF16), vm((width, columns), BF16),
        vm((slots, 1), F32), vm((slots, slots), F32), vm((slots, width), F32), vm((slots, 1), F32),
        vm((slots, width), BF16), vm((2, slots, s.half), BF16),
        vm((slots, columns), BF16), vm((slots, columns), BF16),
        vm((CHUNKS, slots, s.chunk), F32), vm((slots, width), BF16),
        moved, moved, moved, moved,
        vm((columns, s.half), BF16), vm((columns, s.half), F32), vm((columns, s.half), BF16),
        vm((columns, s.half), BF16), vm((s.yh, s.x, s.chip_block, s.half), BF16),
        vm((s.y * s.chip_block, LANES), BF16), vm((s.y * s.chip_block, LANES), BF16),
        vm((s.z * ROWS8, s.chip_block), F32), vm((s.z * ROWS8, s.chip_block), F32),
        vm((ROWS8, s.chip_block), F32), vm((ROWS8, s.chip_block), F32),
        vm((s.c,) + norms, F32), vm((s.x,) + norms, F32), vm((s.y,) + norms, F32),
        vm((s.zb,) + norms, F32), vm((s.za,) + norms, F32),
    ]
    xy = s.x * s.yh
    counts = [len(args), len(outs) + CHUNKS - 1]
    counts += [CHUNKS] * 8
    counts += [1, 1, 1, s.yh, xy, xy, xy, xy]
    counts += [3, 3, s.yh, s.yh] + [1] * 6
    counts += [1] * 10
    scratch += [dma((n,)) for n in counts]
    results = pl.pallas_call(
        functools.partial(kernel, s),
        out_shape=outs,
        in_specs=[whole] * len(args),
        out_specs=(whole,) * len(outs),
        scratch_shapes=scratch,
        compiler_params=pltpu.CompilerParams(
            collective_id=0, has_side_effects=True, vmem_limit_bytes=56 * 1024 * 1024
        ),
        cost_estimate=pl.CostEstimate(
            flops=2_000_000_000, bytes_accessed=3_000_000, transcendentals=400_000
        ),
        name="joint_block",
    )(*args)
    return pl.pallas_call(
        copy_out,
        out_shape=outs,
        in_specs=[whole] * len(outs),
        out_specs=(whole,) * len(outs),
        scratch_shapes=[vm(a.shape, a.dtype) for a in outs] + [dma((len(outs),))] * 2,
        name="copy_out",
    )(*results)


def solution(mesh):
    rows = P(("grp", "fsdp"), None)
    return jax.shard_map(
        shards,
        mesh=mesh,
        in_specs=(rows, rows, rows, rows, rows, P(), P(), P("fsdp", None), rows),
        out_specs=(rows, rows, P("fsdp", "grp"), P(), P()),
        check_vma=False,
    )
```

```python
import functools

import jax
import jax.numpy as jnp
import numpy as np
from jax import lax
from jax.experimental import pallas as pl
from jax.experimental.pallas import tpu as pltpu
from jax.sharding import PartitionSpec as P

HEAD_DIM = 64
EPSILON = 1e-06
MESH = pl.DeviceIdType.MESH
BF16 = jnp.bfloat16
F32 = jnp.float32
ROWS16 = 16
ROWS8 = 8
LANES = 128
THERE = (1, 2, 2, 1)
BACK = (2, 2, 1, 1)
Y_FIRST = (False, True, True, True)
CHUNKS = len(Y_FIRST)
NORM_ROWS = 64
UNNORM_ROWS = 64


class Sizes:
    def __init__(self, grp, fsdp, slots, width, columns):
        self.yh, self.x, self.c = {16: (2, 4, 2), 4: (1, 2, 2), 8: (2, 2, 2)}[grp]
        self.yl = 4 if fsdp == 64 else 2
        self.z = fsdp // self.yl
        self.zb = 4 if self.z == 16 else 2
        self.za = self.z // self.zb
        self.y = self.yh * self.yl
        self.slots, self.width, self.columns = slots, width, columns
        self.inner = columns // 3
        self.per_peer = slots // fsdp
        self.rows = width // fsdp
        self.half_rows = self.rows // 2
        self.col_block = columns // grp
        self.chip_block = self.col_block * self.c
        self.pieces = self.yh * self.x
        sixth = width // 6
        self.cols, self.back_cols = (
            [slice(sixth * sum(parts[:c]), sixth * sum(parts[: c + 1])) for c in range(CHUNKS)]
            for parts in (THERE, BACK)
        )
        self.half = width // 2
        self.z_lanes = self.z * self.half_rows
        self.fold = (columns // LANES * 2 // 9) * LANES
        self.kept = columns - self.fold


def index_rows(s):
    table = np.full((8, max(s.width, s.yl * LANES, s.slots)), -1, np.int32)
    for j in range(s.width):
        h, r = divmod(j, s.half)
        yl, r = divmod(r, s.z_lanes)
        z, i = divmod(r, s.half_rows)
        table[0, j] = (z * s.yl + yl) * s.rows + h * s.half_rows + i
    for yl in range(s.yl):
        for j in range(s.z_lanes):
            table[1, yl * LANES + j] = yl * s.z_lanes + j
    for yl in range(s.yl):
        for z in range(s.z):
            for r in range(s.per_peer):
                q = (yl * s.z + z) * s.per_peer + r
                table[2, q] = (z * s.yl + yl) * s.per_peer + r
    for yl in range(s.yl):
        for i in range(s.rows):
            table[3, yl * ROWS16 + i] = yl * s.rows + i
            table[5 + i % 3, yl * ROWS16 + s.rows + i // 3] = yl * s.rows + i
    for z in range(s.z):
        for i in range(s.half_rows):
            table[4, z * s.half_rows + i] = z * ROWS8 + i
    return table


def one_hot(count, row):
    ids = lax.broadcasted_iota(jnp.int32, (count, row.shape[1]), 0)
    return jnp.where(ids == row, 1.0, 0.0).astype(BF16)


def mm(a, b, dims=((1,), (0,))):
    return lax.dot_general(a, b, (dims, ((), ())), preferred_element_type=F32)


TN = ((0,), (0,))
NT = ((1,), (1,))


def kernel(
    s, tok_h, send_order_h, recv_order_h, row_ids_h, frames_h, gains_h, biases_h, wshard_h, dout_h, table_h,
    attended_h, grad_tokens_h, grad_weight_h, grad_scale_h, grad_shift_h,
    tok, send_order, recv_order, row_ids, frames, gains, biases, wshard, dout, table,
    attended, grad_tokens, grad_weight, grad_scale, grad_shift,
    pt, pt_q, perm, rt, rt_q, feat, a_out, a_in, b_out, b_in, packed, wpad, wsh, wyin, weight,
    aud, same, standard, inv, normed, normed_p, qkv, gqkv, gnorm, gpacked,
    r_out, r_in, t_out, t_in, g_send, g_own, g_in, x_out, x_in, y_out, y_in, z_out, z_in,
    f_send, f_in, n_c, n_x, n_y, n_zb, n_za,
    load, store,
    ya_s, ya_r, za_s, za_r, yb_s, yb_r, zb_s, zb_r,
    wz_s, wz_r, wy_s, wy_r, wx_s, wx_r, wc_s, wc_r,
    gc_s, gc_r, gx_s, gx_r, gy_s, gy_r, gz_s, gz_r, gf_s, gf_r,
    nc_s, nc_r, nx_s, nx_r, ny_s, ny_r, nzb_s, nzb_r, nza_s, nza_r,
):
    g = lax.axis_index("grp")
    f = lax.axis_index("fsdp")
    core = g % s.c
    my_x = (g // s.c) % s.x
    my_yh = g // (s.c * s.x)
    my_z = f // s.yl
    my_yl = f % s.yl
    my_y = my_yh * s.yl + my_yl
    other = 1 - core

    def grp_of(yh, x, c):
        return (yh * s.x + x) * s.c + c

    def at_z(z):
        return (g, z * s.yl + my_yl)

    def at_yl(yl):
        return (g, my_z * s.yl + yl)

    def at_y(y):
        return (grp_of(y // s.yl, my_x, core), my_z * s.yl + y % s.yl)

    def at_x(x):
        return (grp_of(my_yh, x, core), f)

    sibling = (grp_of(my_yh, my_x, other), f)

    def others(count, me, body):
        def step(i, carry):
            body((me + count // 2 + (i + 1) // 2 * (1 - 2 * (i % 2))) % count)
            return carry

        lax.fori_loop(0, count - 1, step, 0)

    def remote(src, dst, send, recv, device):
        return pltpu.make_async_remote_copy(
            src_ref=src, dst_ref=dst, send_sem=send, recv_sem=recv,
            device_id=device, device_id_type=MESH,
        )

    ends = []

    def rows_of(ref, k, count):
        return ref.at[pl.ds(pl.multiple_of(k * count, count), count), :]

    class Exchange:
        def __init__(self, src, dst, rows, count, me, send, recv, at, spread=True):
            self.src, self.dst, self.rows, self.count, self.me = src, dst, rows, count, me
            self.send, self.recv, self.at, self.spread = send, recv, at, spread

        def copy(self, p):
            block = rows_of(self.src, p if self.spread else 0, self.rows)
            return remote(block, rows_of(self.dst, self.me, self.rows), self.send, self.recv, self.at(p))

        def start(self):
            others(self.count, self.me, lambda p: self.copy(p).start())
            self.started()

        def start_one(self, p):
            @pl.when(p != self.me)
            def _():
                self.copy(p).start()

        def started(self):
            ends.append(self.whole().wait_send)
            mine = rows_of(self.src, self.me if self.spread else 0, self.rows)
            rows_of(self.dst, self.me, self.rows)[...] = mine[...]

        def whole(self):
            part = self.dst.at[pl.ds(0, (self.count - 1) * self.rows), :]
            return remote(part, part, self.send, self.recv, self.at((self.me + 1) % self.count))

        def wait(self):
            self.whole().wait_recv()

    barrier = pltpu.get_barrier_semaphore()

    def greet(device):
        pl.semaphore_signal(barrier, inc=1, device_id=device, device_id_type=MESH)

    others(s.z, my_z, lambda z: greet(at_z(z)))
    others(s.y, my_y, lambda y: greet(at_y(y)))
    others(s.x, my_x, lambda x: greet(at_x(x)))
    greet(sibling)

    inputs = [
        (send_order_h, send_order), (table_h, table), (tok_h, tok), (wshard_h, wshard), (recv_order_h, recv_order),
        (row_ids_h, row_ids), (frames_h, frames), (gains_h, gains), (biases_h, biases), (dout_h, dout),
    ]
    loads = [pltpu.make_async_copy(src, dst, load.at[i]) for i, (src, dst) in enumerate(inputs)]
    for copy in loads:
        copy.start()

    for copy in loads:
        copy.wait()
    to_q = one_hot(s.slots, table[2:3, : s.slots])
    perm[...] = to_q
    pt[...] = one_hot(s.slots, send_order[...])
    pt_q[...] = mm(pt[...], to_q).astype(BF16)
    rt[...] = one_hot(s.slots, recv_order[...])
    rt_q[...] = mm(to_q, rt[...], TN).astype(BF16)
    wpad[...] = jnp.zeros_like(wpad)
    wpad[0 : s.rows, :] = wshard[:, : s.kept]
    for k in range(3 if s.fold else 0):
        down_rows = one_hot(s.rows, table[5 + k : 6 + k, :ROWS16])
        folded = mm(down_rows, wshard[:, s.kept :], TN).astype(BF16)
        wpad[:, k * s.fold : (k + 1) * s.fold] += folded
    for c in range(CHUNKS):
        a_out[c][...] = mm((pt_q if Y_FIRST[c] else pt)[...], tok[:, s.cols[c]], TN).astype(BF16)
    pl.semaphore_wait(barrier, (s.z - 1) + (s.y - 1) + (s.x - 1) + 1)

    run = s.slots // s.yl
    block = s.slots // s.z

    def along(y, out, into, send, recv, c):
        if y:
            return Exchange(out[c], into[c], run, s.yl, my_yl, send.at[c], recv.at[c], at_yl)
        return Exchange(out[c], into[c], block, s.z, my_z, send.at[c], recv.at[c], at_z)

    def turned(c, value):
        return mm(perm[...], value, ((1,), (0,)) if Y_FIRST[c] else TN).astype(BF16)

    first_1 = [along(Y_FIRST[c], a_out, a_in, ya_s, ya_r, c) for c in range(CHUNKS)]
    first_2 = [along(not Y_FIRST[c], b_out, b_in, za_s, za_r, c) for c in range(CHUNKS)]
    back_1 = [along(Y_FIRST[c], r_out, r_in, yb_s, yb_r, c) for c in range(CHUNKS)]
    back_2 = [along(not Y_FIRST[c], t_out, t_in, zb_s, zb_r, c) for c in range(CHUNKS)]

    def wz_copy(z):
        return remote(wpad, wsh, wz_s.at[0], wz_r.at[0], at_z(z))

    @pl.when(my_z == g)
    def _():
        others(s.z, my_z, lambda z: wz_copy(z).start())
        wsh[...] = wpad[...]

    for c in range(CHUNKS):
        first_1[c].start()

    def first_turn(c):
        first_1[c].wait()
        b_out[c][...] = turned(c, a_in[c][...])
        first_2[c].start()

    feat[...] = one_hot(s.width, table[0:1, : s.width])
    ids = row_ids[...].astype(F32)
    down = lax.broadcasted_iota(jnp.int32, (s.slots, s.slots), 0)
    across = lax.broadcasted_iota(jnp.int32, (s.slots, s.slots), 1)
    id_col = jnp.sum(jnp.where(down == across, ids, 0.0), axis=1, keepdims=True)
    before = jnp.sum(jnp.where(ids < id_col, 1.0, 0.0), axis=1, keepdims=True)
    place = lax.broadcasted_iota(jnp.int32, (s.slots, 1), 0).astype(F32) - before
    limit = jnp.zeros((s.slots, 1), F32)
    for k in range(frames.shape[1]):
        limit = limit + jnp.where(id_col == k, frames[0:1, k : k + 1].astype(F32), 0.0)
    aud[...] = jnp.where(place >= limit, 1.0, 0.0)
    same[...] = jnp.where(ids == id_col, 0.0, -1e30)

    wide = s.yl * s.rows
    pick = one_hot(wide, table[3:4, : s.yl * ROWS16])

    def w_rows(yh, x, c):
        return rows_of(weight, grp_of(yh, x, c), wide)

    def wx_copy(yh, x, slot):
        rows = w_rows(yh, slot, core)
        return remote(rows, rows, wx_s.at[x * s.yh + yh], wx_r.at[slot * s.yh + yh], at_x(x))

    def wc_copy(yh, x, c):
        rows = w_rows(yh, x, c)
        return remote(rows, rows, wc_s.at[x * s.yh + yh], wc_r.at[x * s.yh + yh], sibling)

    @pl.when(my_z != g)
    def _():
        wz_copy((my_z + 1) % s.z).wait_recv()

    def wy_copy(y):
        slot = rows_of(wyin, my_y, ROWS16)
        return remote(wsh, slot, wy_s.at[0], wy_r.at[my_yh], at_y(y))

    def wy_part(at, count, send, recv):
        part = wyin.at[pl.ds(at, count * ROWS16), :]
        return remote(part, part, send, recv, at_y((my_y + 1) % s.y))

    others(s.y, my_y, lambda y: wy_copy(y).start())
    ends.append(wy_part(0, s.y - 1, wy_s.at[0], wy_r.at[0]).wait_send)
    rows_of(wyin, my_y, ROWS16)[...] = wsh[...]
    for c in range(1, CHUNKS):
        first_turn(c)

    run16 = s.yl * ROWS16
    for step in range(s.yh):
        yh = (my_yh + step) % s.yh
        wy_part(0, s.yl - 1 if step == 0 else s.yl, wy_s.at[0], wy_r.at[yh]).wait_recv()
        shards_of = wyin[pl.ds(pl.multiple_of(yh * run16, run16), run16), :]
        w_block = w_rows(yh, my_x, core)
        w_block[:, 0 : s.kept] = mm(pick, shards_of).astype(BF16)
        if s.fold:
            w_block[:, s.kept :] = sum(
                mm(one_hot(wide, table[5 + k : 6 + k, : s.yl * ROWS16]), shards_of[:, k * s.fold : (k + 1) * s.fold])
                for k in range(3)
            ).astype(BF16)
        others(s.x, my_x, lambda x, yh=yh: wx_copy(yh, x, my_x).start())
        wc_copy(yh, my_x, core).start()

    first_turn(0)

    def unpack(c):
        first_2[c].wait()
        place_in = rt if Y_FIRST[c] else rt_q
        packed[:, s.cols[c]] = mm(place_in[...], b_in[c][...], TN).astype(BF16)

    def pass_on(step):
        yh = (my_yh + step) % s.yh

        def one(x):
            wx_copy(yh, x, x).wait_recv()
            wc_copy(yh, x, core).start()

        others(s.x, my_x, one)

    unpack(0)
    unpack(1)
    for step in range(s.yh - 1):
        pass_on(step)
    unpack(2)
    unpack(3)

    def by_rows(step_rows, body):
        def step(i, carry):
            body(pl.ds(pl.multiple_of(i * step_rows, step_rows), step_rows))
            return carry

        lax.fori_loop(0, s.slots // step_rows, step, 0)

    def norm(rows):
        values = packed[rows, :].astype(F32)
        centered = values - jnp.mean(values, axis=1, keepdims=True)
        variance = jnp.mean(centered * centered, axis=1, keepdims=True)
        inverse = lax.rsqrt(variance + EPSILON)
        unit = centered * inverse
        inv[rows, :] = inverse
        standard[rows, :] = unit
        audio = jnp.broadcast_to(aud[rows, :], unit.shape) > 0.5
        gain = jnp.where(audio, gains[1:2, :], gains[0:1, :])
        bias = jnp.where(audio, biases[1:2, :], biases[0:1, :])
        normed[rows, :] = (unit * gain + bias).astype(BF16)

    by_rows(NORM_ROWS, norm)
    pass_on(s.yh - 1)
    for h in range(2):
        normed_p[h] = mm(normed[...], feat[:, h * s.half : (h + 1) * s.half]).astype(BF16)

    def wc_all(body):
        for x in range(s.x):
            for yh in range(s.yh):
                body(wc_copy(yh, x, other))

    wc_all(lambda copy: copy.wait_recv())

    def project(i, carry):
        cols = pl.ds(pl.multiple_of(i * s.inner, LANES), s.inner)
        qkv[:, cols] = mm(normed[...], weight[:, cols]).astype(BF16)
        return carry

    lax.fori_loop(0, 3, project, 0, unroll=True)

    pair = 2 * HEAD_DIM
    scaling = 1.0 / HEAD_DIM**0.5

    def heads(i, carry):
        def part(k):
            return pl.ds(pl.multiple_of(k * s.inner + i * pair, LANES), pair)

        lane = lax.broadcasted_iota(jnp.int32, (1, pair), 1)
        masks = [jnp.where(lane < HEAD_DIM, 1.0, 0.0), jnp.where(lane < HEAD_DIM, 0.0, 1.0)]
        q, k, v, do = qkv[:, part(0)], qkv[:, part(1)], qkv[:, part(2)], dout[:, part(0)]

        def split(a):
            return [a * m.astype(BF16) for m in masks]

        qs, ks, vs, dos = split(q), split(k), split(v), split(do)
        probs = []
        for a in range(2):
            scores = mm(qs[a], k, NT) * scaling + same[...]
            exponent = jnp.exp(scores - jnp.max(scores, axis=1, keepdims=True))
            probs.append((exponent * (1.0 / jnp.sum(exponent, axis=1, keepdims=True))).astype(BF16))
        out = mm(jnp.concatenate(probs, axis=1), jnp.concatenate(vs, axis=0)).astype(BF16)
        attended[:, part(0)] = out
        delta = do.astype(F32) * out.astype(F32)
        grads = []
        for a in range(2):
            row_delta = jnp.sum(delta * masks[a], axis=1, keepdims=True)
            grad_probs = mm(dos[a], v, NT)
            grads.append((probs[a].astype(F32) * (grad_probs - row_delta) * scaling).astype(BF16))
        gqkv[:, part(0)] = mm(
            jnp.concatenate(grads, axis=1), jnp.concatenate(ks, axis=0)
        ).astype(BF16)
        gqkv[:, part(1)] = mm(
            jnp.concatenate(grads, axis=0), jnp.concatenate(qs, axis=0), TN
        ).astype(BF16)
        gqkv[:, part(2)] = mm(
            jnp.concatenate(probs, axis=0), jnp.concatenate(dos, axis=0), TN
        ).astype(BF16)
        return carry

    lax.fori_loop(0, s.inner // pair, heads, 0, unroll=True)
    stores = []

    def keep(src, dst):
        copy = pltpu.make_async_copy(src, dst, store.at[len(stores)])
        copy.start()
        stores.append(copy)

    keep(attended, attended_h)

    third = s.columns // 3

    def third_rows(k):
        return pl.ds(k * third, third)

    def gc_copy(k):
        return remote(g_send.at[third_rows(k), :], g_in.at[third_rows(k), :], gc_s.at[k], gc_r.at[k], sibling)

    for k in range(3):
        g_send[third_rows(k), :] = mm(gqkv[:, k * third : (k + 1) * third], normed_p[other], TN).astype(BF16)
        gc_copy(k).start()
        ends.append(gc_copy(k).wait_send)

    for k in range(3):
        rows = slice(k * s.width // 3, (k + 1) * s.width // 3)
        gnorm[:, rows] = mm(gqkv[...], weight[rows, :], NT)
    def piece_rows(p):
        return pl.ds(pl.multiple_of(p * s.chip_block, ROWS16), s.chip_block)

    def gx_copy(yh, x, slot):
        return remote(x_out.at[piece_rows(yh * s.x + x), :], x_in.at[yh, slot], gx_s.at[yh], gx_r.at[yh], at_x(x))

    sent = 0
    for k in range(3):
        g_own[third_rows(k), :] = mm(gqkv[:, k * third : (k + 1) * third], normed_p[core], TN)
        gc_copy(k).wait_recv()
        both = g_own[third_rows(k), :] + g_in[third_rows(k), :].astype(F32)
        g_own[third_rows(k), :] = both
        x_out[third_rows(k), :] = both.astype(BF16)
        while (sent + 1) * s.chip_block <= (k + 1) * third:
            yh, x = sent // s.x, sent % s.x

            @pl.when(x != my_x)
            def _(yh=yh, x=x):
                gx_copy(yh, x, my_x).start()

            sent += 1
    gx_all = []
    for yh in range(s.yh):
        part = x_in.at[yh, pl.ds(0, s.x - 1)]
        gx_all.append(remote(part, part, gx_s.at[yh], gx_r.at[yh], at_x((my_x + 1) % s.x)))
        ends.append(gx_all[yh].wait_send)

    my_za, my_zb = my_z // s.zb, my_z % s.zb
    n_zb[my_zb] = jnp.zeros_like(n_zb[0])

    def unnorm(rows):
        grad = gnorm[rows, :]
        unit = standard[rows, :]
        audio = jnp.broadcast_to(aud[rows, :], unit.shape) > 0.5
        gain = jnp.where(audio, gains[1:2, :], gains[0:1, :])
        gain_term = grad * unit
        n_zb[my_zb] += jnp.concatenate(
            [
                jnp.sum(jnp.where(audio, 0.0, gain_term), axis=0, keepdims=True),
                jnp.sum(jnp.where(audio, gain_term, 0.0), axis=0, keepdims=True),
                jnp.sum(jnp.where(audio, 0.0, grad), axis=0, keepdims=True),
                jnp.sum(jnp.where(audio, grad, 0.0), axis=0, keepdims=True),
            ],
            axis=0,
        )
        scaled = grad * gain
        out = inv[rows, :] * (
            scaled
            - jnp.mean(scaled, axis=1, keepdims=True)
            - unit * jnp.mean(scaled * unit, axis=1, keepdims=True)
        )
        gpacked[rows, :] = out.astype(BF16)

    by_rows(UNNORM_ROWS, unnorm)

    def total(buf, count):
        result = buf[0]
        for k in range(1, count):
            result = result + buf[k]
        return result

    class Sum:
        def __init__(self, buf, count, me, send, recv, at):
            self.buf, self.count, self.me, self.at = buf, count, me, at
            self.send, self.recv = send.at[0], recv.at[0]

        def start(self, value=None):
            if value is not None:
                self.buf[self.me] = value
            mine = self.buf.at[self.me]
            others(self.count, self.me, lambda p: remote(mine, mine, self.send, self.recv, self.at(p)).start())
            ends.append(self.whole().wait_send)

        def whole(self):
            part = self.buf.at[pl.ds(0, self.count - 1)]
            return remote(part, part, self.send, self.recv, self.at((self.me + 1) % self.count))

        def result(self):
            self.whole().wait_recv()
            return total(self.buf, self.count)

    sum_zb = Sum(n_zb, s.zb, my_zb, nzb_s, nzb_r, lambda zb: at_z(my_za * s.zb + zb))
    sum_za = Sum(n_za, s.za, my_za, nza_s, nza_r, lambda za: at_z(za * s.zb + my_zb))
    sum_c = Sum(n_c, s.c, core, nc_s, nc_r, lambda c: (grp_of(my_yh, my_x, c), f))
    sum_y = Sum(n_y, s.y, my_y, ny_s, ny_r, at_y)
    sum_x = Sum(n_x, s.x, my_x, nx_s, nx_r, at_x)
    sum_zb.start()

    for c in (1, 0, 2, 3):
        place_in = rt_q if Y_FIRST[c] else rt
        r_out[c][...] = mm(place_in[...], gpacked[:, s.back_cols[c]]).astype(BF16)
        if c < 2:
            back_1[c].start()

    def back_turn(c):
        back_1[c].wait()
        t_out[c][...] = turned(c, r_in[c][...])
        back_2[c].start()

    sum_c.start(sum_zb.result())
    back_turn(1)
    back_1[2].start()
    back_1[3].start()
    sum_x.start(sum_c.result())

    spread = one_hot(s.half, table[1:2, : s.yl * LANES])
    gy = Exchange(y_out, y_in, s.chip_block, s.y, my_y, gy_s.at[0], gy_r.at[0], at_y)
    for yh in range(s.yh):
        gx_all[yh].wait_recv()
        piece = g_own[piece_rows(yh * s.x + my_x), :]
        for step in range(1, s.x):
            piece = piece + x_in[yh, (my_x + step) % s.x].astype(F32)
        wide_piece = mm(piece.astype(BF16), spread).astype(BF16)
        for yl in range(s.yl):
            at = (yh * s.yl + yl) * s.chip_block
            y_out[at : at + s.chip_block, :] = wide_piece[:, yl * LANES : (yl + 1) * LANES]
            gy.start_one(yh * s.yl + yl)
        if yh == 0:
            back_turn(2)
    gy.started()
    sum_za.start(sum_x.result())
    back_turn(3)
    back_turn(0)

    gy.wait()
    piece = y_in[0 : s.chip_block, :].astype(F32)
    for y in range(1, s.y):
        piece = piece + y_in[y * s.chip_block : (y + 1) * s.chip_block, :].astype(F32)
    apart = one_hot(s.z * ROWS8, table[4:5, :LANES])
    z_out[...] = mm(apart, piece.astype(BF16), NT)
    gz = Exchange(z_out, z_in, ROWS8, s.z, my_z, gz_s.at[0], gz_r.at[0], at_z)
    gz.start()
    sum_y.start(sum_za.result())

    def home(c):
        back_2[c].wait()
        grad_tokens[c][...] = mm((pt if Y_FIRST[c] else pt_q)[...], t_in[c][...]).astype(BF16)
        cols = s.back_cols[c]
        keep(grad_tokens[c], grad_tokens_h.at[:, pl.ds(cols.start, cols.stop - cols.start)])

    home(0)
    home(1)
    home(2)

    @pl.when(my_z == g)
    def _():
        part = weight.at[pl.ds(0, (s.z - 1) * ROWS16), pl.ds(0, s.kept)]
        remote(part, part, wz_s.at[0], wz_r.at[0], at_z((my_z + 1) % s.z)).wait_send()

    others(s.x, my_x, lambda x: [wx_copy(yh, x, my_x).wait_send() for yh in range(s.yh)])
    wc_all(lambda copy: copy.wait_send())
    for wait in ends[:-2]:
        wait()
    last_ends = ends[-2:]
    del ends[:]
    gz.wait()
    own = z_in[0:ROWS8, :]
    for z in range(1, s.z):
        own = own + z_in[z * ROWS8 : (z + 1) * ROWS8, :]
    f_send[...] = own
    f_copy = remote(f_send, f_in, gf_s.at[0], gf_r.at[0], sibling)
    f_copy.start()
    ends.append(f_copy.wait_send)
    home(3)
    norms = sum_y.result()
    grad_scale[...] = norms[0:2]
    grad_shift[...] = norms[2:4]
    keep(grad_scale, grad_scale_h)
    keep(grad_shift, grad_shift_h)
    f_copy.wait_recv()
    first = core == 0
    theirs = f_in[...]
    low, high = jnp.where(first, own, theirs), jnp.where(first, theirs, own)
    for at, value in ((0, low), (s.half_rows, high)):
        mine = jnp.where(first, value[:, : s.col_block], value[:, s.col_block :])
        grad_weight[at : at + s.half_rows, :] = mine[: s.half_rows]
    keep(grad_weight, grad_weight_h)

    for wait in last_ends + ends:
        wait()
    for copy in stores:
        copy.wait()


def copy_out(*refs):
    count = (len(refs) - 2) // 3
    sources, targets, held = refs[:count], refs[count : 2 * count], refs[2 * count : 3 * count]
    load, store = refs[3 * count :]
    loads = [pltpu.make_async_copy(sources[i], held[i], load.at[i]) for i in range(count)]
    stores = [pltpu.make_async_copy(held[i], targets[i], store.at[i]) for i in range(count)]
    for copy in loads:
        copy.start()
    for i in range(count):
        loads[i].wait()
        stores[i].start()
    for copy in stores:
        copy.wait()


def shards(
    tokens, send_order, recv_order, row_ids, frames, norm_scale, norm_shift, qkv_weight, d_out
):
    slots, width = tokens.shape
    columns = qkv_weight.shape[1]
    s = Sizes(lax.axis_size("grp"), lax.axis_size("fsdp"), slots, width, columns)
    whole = pl.BlockSpec(memory_space=pl.ANY)
    vm, dma = pltpu.VMEM, pltpu.SemaphoreType.DMA
    there, back = (
        [vm((slots, cols.stop - cols.start), BF16) for cols in parts] for parts in (s.cols, s.back_cols)
    )
    norms = (4, width)
    args = (
        tokens, send_order, recv_order, row_ids, frames, norm_scale, norm_shift, qkv_weight, d_out,
        jnp.asarray(index_rows(s)),
    )
    sds = jax.ShapeDtypeStruct
    outs = (
        sds((slots, s.inner), BF16), sds((slots, width), BF16),
        sds((s.rows, s.col_block), F32), sds((2, width), F32), sds((2, width), F32),
    )
    scratch = [vm(a.shape, a.dtype) for a in args]
    scratch += [vm((slots, s.inner), BF16), back]
    scratch += [vm(a.shape, a.dtype) for a in outs[2:]]
    scratch += [
        vm((slots, slots), BF16), vm((slots, slots), BF16), vm((slots, slots), BF16),
        vm((slots, slots), BF16), vm((slots, slots), BF16),
        vm((width, width), BF16), there, there, there, there, vm((slots, width), BF16),
        vm((ROWS16, s.kept), BF16), vm((ROWS16, s.kept), BF16),
        vm((s.y * ROWS16, s.kept), BF16), vm((width, columns), BF16),
        vm((slots, 1), F32), vm((slots, slots), F32), vm((slots, width), F32), vm((slots, 1), F32),
        vm((slots, width), BF16), vm((2, slots, s.half), BF16),
        vm((slots, columns), BF16), vm((slots, columns), BF16),
        vm((slots, width), F32), vm((slots, width), BF16),
        back, back, back, back,
        vm((columns, s.half), BF16), vm((columns, s.half), F32), vm((columns, s.half), BF16),
        vm((columns, s.half), BF16), vm((s.yh, s.x, s.chip_block, s.half), BF16),
        vm((s.y * s.chip_block, LANES), BF16), vm((s.y * s.chip_block, LANES), BF16),
        vm((s.z * ROWS8, s.chip_block), F32), vm((s.z * ROWS8, s.chip_block), F32),
        vm((ROWS8, s.chip_block), F32), vm((ROWS8, s.chip_block), F32),
        vm((s.c,) + norms, F32), vm((s.x,) + norms, F32), vm((s.y,) + norms, F32),
        vm((s.zb,) + norms, F32), vm((s.za,) + norms, F32),
    ]
    xy = s.x * s.yh
    counts = [len(args), len(outs) + CHUNKS - 1]
    counts += [CHUNKS] * 8
    counts += [1, 1, 1, s.yh, xy, xy, xy, xy]
    counts += [3, 3, s.yh, s.yh] + [1] * 6
    counts += [1] * 10
    scratch += [dma((n,)) for n in counts]
    results = pl.pallas_call(
        functools.partial(kernel, s),
        out_shape=outs,
        in_specs=[whole] * len(args),
        out_specs=(whole,) * len(outs),
        scratch_shapes=scratch,
        compiler_params=pltpu.CompilerParams(
            collective_id=0, has_side_effects=True, vmem_limit_bytes=56 * 1024 * 1024
        ),
        cost_estimate=pl.CostEstimate(
            flops=2_000_000_000, bytes_accessed=3_000_000, transcendentals=400_000
        ),
        name="joint_block",
    )(*args)
    return pl.pallas_call(
        copy_out,
        out_shape=outs,
        in_specs=[whole] * len(outs),
        out_specs=(whole,) * len(outs),
        scratch_shapes=[vm(a.shape, a.dtype) for a in outs] + [dma((len(outs),))] * 2,
        name="copy_out",
    )(*results)


def solution(mesh):
    rows = P(("grp", "fsdp"), None)
    return jax.shard_map(
        shards,
        mesh=mesh,
        in_specs=(rows, rows, rows, rows, rows, P(), P(), P("fsdp", None), rows),
        out_specs=(rows, rows, P("fsdp", "grp"), P(), P()),
        check_vma=False,
    )
```

```python
import functools

import jax
import jax.numpy as jnp
import numpy as np
from jax import lax
from jax.experimental import pallas as pl
from jax.experimental.pallas import tpu as pltpu
from jax.sharding import PartitionSpec as P

HEAD_DIM = 64
EPSILON = 1e-06
MESH = pl.DeviceIdType.MESH
BF16 = jnp.bfloat16
F32 = jnp.float32
ROWS16 = 16
ROWS8 = 8
LANES = 128
THERE = (1, 2, 2, 1)
BACK = (2, 2, 1, 1)
Y_FIRST = (False, True, True, True)
CHUNKS = len(Y_FIRST)
NORM_ROWS = 64
UNNORM_ROWS = 64


class Sizes:
    def __init__(self, grp, fsdp, slots, width, columns):
        self.yh, self.x, self.c = {16: (2, 4, 2), 4: (1, 2, 2), 8: (2, 2, 2)}[grp]
        self.yl = 4 if fsdp == 64 else 2
        self.z = fsdp // self.yl
        self.zb = 4 if self.z == 16 else 2
        self.za = self.z // self.zb
        self.y = self.yh * self.yl
        self.slots, self.width, self.columns = slots, width, columns
        self.inner = columns // 3
        self.per_peer = slots // fsdp
        self.rows = width // fsdp
        self.half_rows = self.rows // 2
        self.col_block = columns // grp
        self.chip_block = self.col_block * self.c
        self.pieces = self.yh * self.x
        sixth = width // 6
        self.cols, self.back_cols = (
            [slice(sixth * sum(parts[:c]), sixth * sum(parts[: c + 1])) for c in range(CHUNKS)]
            for parts in (THERE, BACK)
        )
        self.half = width // 2
        self.z_lanes = self.z * self.half_rows
        self.fold = (columns // LANES * 2 // 9) * LANES
        self.kept = columns - self.fold


def index_rows(s):
    table = np.full((8, max(s.width, s.yl * LANES, s.slots)), -1, np.int32)
    for j in range(s.width):
        h, r = divmod(j, s.half)
        yl, r = divmod(r, s.z_lanes)
        z, i = divmod(r, s.half_rows)
        table[0, j] = (z * s.yl + yl) * s.rows + h * s.half_rows + i
    for yl in range(s.yl):
        for j in range(s.z_lanes):
            table[1, yl * LANES + j] = yl * s.z_lanes + j
    for yl in range(s.yl):
        for z in range(s.z):
            for r in range(s.per_peer):
                q = (yl * s.z + z) * s.per_peer + r
                table[2, q] = (z * s.yl + yl) * s.per_peer + r
    for yl in range(s.yl):
        for i in range(s.rows):
            table[3, yl * ROWS16 + i] = yl * s.rows + i
            table[5 + i % 3, yl * ROWS16 + s.rows + i // 3] = yl * s.rows + i
    for z in range(s.z):
        for i in range(s.half_rows):
            table[4, z * s.half_rows + i] = z * ROWS8 + i
    return table


def one_hot(count, row):
    ids = lax.broadcasted_iota(jnp.int32, (count, row.shape[1]), 0)
    return jnp.where(ids == row, 1.0, 0.0).astype(BF16)


def mm(a, b, dims=((1,), (0,))):
    return lax.dot_general(a, b, (dims, ((), ())), preferred_element_type=F32)


TN = ((0,), (0,))
NT = ((1,), (1,))


def kernel(
    s, tok_h, send_order_h, recv_order_h, row_ids_h, frames_h, gains_h, biases_h, wshard_h, dout_h, table_h,
    attended_h, grad_tokens_h, grad_weight_h, grad_scale_h, grad_shift_h,
    tok, send_order, recv_order, row_ids, frames, gains, biases, wshard, dout, table,
    attended, grad_tokens, grad_weight, grad_scale, grad_shift,
    pt, pt_q, perm, rt, rt_q, feat, a_out, a_in, b_out, b_in, packed, wpad, wsh, wyin, weight,
    aud, same, standard, inv, normed, normed_p, qkv, gqkv, gnorm, gpacked,
    r_out, r_in, t_out, t_in, g_send, g_own, g_in, x_out, x_in, y_out, y_in, z_out, z_in,
    f_send, f_in, n_c, n_x, n_y, n_zb, n_za,
    load, store,
    ya_s, ya_r, za_s, za_r, yb_s, yb_r, zb_s, zb_r,
    wz_s, wz_r, wy_s, wy_r, wx_s, wx_r, wc_s, wc_r,
    gc_s, gc_r, gx_s, gx_r, gy_s, gy_r, gz_s, gz_r, gf_s, gf_r,
    nc_s, nc_r, nx_s, nx_r, ny_s, ny_r, nzb_s, nzb_r, nza_s, nza_r,
):
    g = lax.axis_index("grp")
    f = lax.axis_index("fsdp")
    core = g % s.c
    my_x = (g // s.c) % s.x
    my_yh = g // (s.c * s.x)
    my_z = f // s.yl
    my_yl = f % s.yl
    my_y = my_yh * s.yl + my_yl
    other = 1 - core

    def grp_of(yh, x, c):
        return (yh * s.x + x) * s.c + c

    def at_z(z):
        return (g, z * s.yl + my_yl)

    def at_yl(yl):
        return (g, my_z * s.yl + yl)

    def at_y(y):
        return (grp_of(y // s.yl, my_x, core), my_z * s.yl + y % s.yl)

    def at_x(x):
        return (grp_of(my_yh, x, core), f)

    sibling = (grp_of(my_yh, my_x, other), f)

    def others(count, me, body):
        def step(i, carry):
            body((me + count // 2 + (i + 1) // 2 * (1 - 2 * (i % 2))) % count)
            return carry

        lax.fori_loop(0, count - 1, step, 0)

    def remote(src, dst, send, recv, device):
        return pltpu.make_async_remote_copy(
            src_ref=src, dst_ref=dst, send_sem=send, recv_sem=recv,
            device_id=device, device_id_type=MESH,
        )

    ends = []

    def rows_of(ref, k, count):
        return ref.at[pl.ds(pl.multiple_of(k * count, count), count), :]

    class Exchange:
        def __init__(self, src, dst, rows, count, me, send, recv, at, spread=True):
            self.src, self.dst, self.rows, self.count, self.me = src, dst, rows, count, me
            self.send, self.recv, self.at, self.spread = send, recv, at, spread

        def copy(self, p):
            block = rows_of(self.src, p if self.spread else 0, self.rows)
            return remote(block, rows_of(self.dst, self.me, self.rows), self.send, self.recv, self.at(p))

        def start(self):
            others(self.count, self.me, lambda p: self.copy(p).start())
            self.started()

        def start_one(self, p):
            @pl.when(p != self.me)
            def _():
                self.copy(p).start()

        def started(self):
            ends.append(self.whole().wait_send)
            mine = rows_of(self.src, self.me if self.spread else 0, self.rows)
            rows_of(self.dst, self.me, self.rows)[...] = mine[...]

        def whole(self):
            part = self.dst.at[pl.ds(0, (self.count - 1) * self.rows), :]
            return remote(part, part, self.send, self.recv, self.at((self.me + 1) % self.count))

        def wait(self):
            self.whole().wait_recv()

    barrier = pltpu.get_barrier_semaphore()

    def greet(device):
        pl.semaphore_signal(barrier, inc=1, device_id=device, device_id_type=MESH)

    others(s.z, my_z, lambda z: greet(at_z(z)))
    others(s.y, my_y, lambda y: greet(at_y(y)))
    others(s.x, my_x, lambda x: greet(at_x(x)))
    greet(sibling)

    inputs = [
        (send_order_h, send_order), (table_h, table), (tok_h, tok), (wshard_h, wshard), (recv_order_h, recv_order),
        (row_ids_h, row_ids), (frames_h, frames), (gains_h, gains), (biases_h, biases), (dout_h, dout),
    ]
    loads = [pltpu.make_async_copy(src, dst, load.at[i]) for i, (src, dst) in enumerate(inputs)]
    for copy in loads:
        copy.start()

    for copy in loads:
        copy.wait()
    to_q = one_hot(s.slots, table[2:3, : s.slots])
    perm[...] = to_q
    pt[...] = one_hot(s.slots, send_order[...])
    pt_q[...] = mm(pt[...], to_q).astype(BF16)
    rt[...] = one_hot(s.slots, recv_order[...])
    rt_q[...] = mm(to_q, rt[...], TN).astype(BF16)
    wpad[...] = jnp.zeros_like(wpad)
    wpad[0 : s.rows, :] = wshard[:, : s.kept]
    for k in range(3 if s.fold else 0):
        down_rows = one_hot(s.rows, table[5 + k : 6 + k, :ROWS16])
        folded = mm(down_rows, wshard[:, s.kept :], TN).astype(BF16)
        wpad[:, k * s.fold : (k + 1) * s.fold] += folded
    for c in range(CHUNKS):
        a_out[c][...] = mm((pt_q if Y_FIRST[c] else pt)[...], tok[:, s.cols[c]], TN).astype(BF16)
    pl.semaphore_wait(barrier, (s.z - 1) + (s.y - 1) + (s.x - 1) + 1)

    run = s.slots // s.yl
    block = s.slots // s.z

    def along(y, out, into, send, recv, c):
        if y:
            return Exchange(out[c], into[c], run, s.yl, my_yl, send.at[c], recv.at[c], at_yl)
        return Exchange(out[c], into[c], block, s.z, my_z, send.at[c], recv.at[c], at_z)

    def turned(c, value):
        return mm(perm[...], value, ((1,), (0,)) if Y_FIRST[c] else TN).astype(BF16)

    first_1 = [along(Y_FIRST[c], a_out, a_in, ya_s, ya_r, c) for c in range(CHUNKS)]
    first_2 = [along(not Y_FIRST[c], b_out, b_in, za_s, za_r, c) for c in range(CHUNKS)]
    back_1 = [along(Y_FIRST[c], r_out, r_in, yb_s, yb_r, c) for c in range(CHUNKS)]
    back_2 = [along(not Y_FIRST[c], t_out, t_in, zb_s, zb_r, c) for c in range(CHUNKS)]

    def wz_copy(z):
        return remote(wpad, wsh, wz_s.at[0], wz_r.at[0], at_z(z))

    @pl.when(my_z == g)
    def _():
        others(s.z, my_z, lambda z: wz_copy(z).start())
        wsh[...] = wpad[...]

    for c in range(CHUNKS):
        first_1[c].start()

    def first_turn(c):
        first_1[c].wait()
        b_out[c][...] = turned(c, a_in[c][...])
        first_2[c].start()

    feat[...] = one_hot(s.width, table[0:1, : s.width])
    ids = row_ids[...].astype(F32)
    down = lax.broadcasted_iota(jnp.int32, (s.slots, s.slots), 0)
    across = lax.broadcasted_iota(jnp.int32, (s.slots, s.slots), 1)
    id_col = jnp.sum(jnp.where(down == across, ids, 0.0), axis=1, keepdims=True)
    before = jnp.sum(jnp.where(ids < id_col, 1.0, 0.0), axis=1, keepdims=True)
    place = lax.broadcasted_iota(jnp.int32, (s.slots, 1), 0).astype(F32) - before
    limit = jnp.zeros((s.slots, 1), F32)
    for k in range(frames.shape[1]):
        limit = limit + jnp.where(id_col == k, frames[0:1, k : k + 1].astype(F32), 0.0)
    aud[...] = jnp.where(place >= limit, 1.0, 0.0)
    same[...] = jnp.where(ids == id_col, 0.0, -1e30)

    wide = s.yl * s.rows
    pick = one_hot(wide, table[3:4, : s.yl * ROWS16])

    def w_rows(yh, x, c):
        return rows_of(weight, grp_of(yh, x, c), wide)

    def wx_copy(yh, x, slot):
        rows = w_rows(yh, slot, core)
        return remote(rows, rows, wx_s.at[x * s.yh + yh], wx_r.at[slot * s.yh + yh], at_x(x))

    def wc_copy(yh, x, c):
        rows = w_rows(yh, x, c)
        return remote(rows, rows, wc_s.at[x * s.yh + yh], wc_r.at[x * s.yh + yh], sibling)

    @pl.when(my_z != g)
    def _():
        wz_copy((my_z + 1) % s.z).wait_recv()

    def wy_copy(y):
        slot = rows_of(wyin, my_y, ROWS16)
        return remote(wsh, slot, wy_s.at[0], wy_r.at[my_yh], at_y(y))

    def wy_part(at, count, send, recv):
        part = wyin.at[pl.ds(at, count * ROWS16), :]
        return remote(part, part, send, recv, at_y((my_y + 1) % s.y))

    others(s.y, my_y, lambda y: wy_copy(y).start())
    ends.append(wy_part(0, s.y - 1, wy_s.at[0], wy_r.at[0]).wait_send)
    rows_of(wyin, my_y, ROWS16)[...] = wsh[...]
    for c in range(1, CHUNKS):
        first_turn(c)

    run16 = s.yl * ROWS16
    for step in range(s.yh):
        yh = (my_yh + step) % s.yh
        wy_part(0, s.yl - 1 if step == 0 else s.yl, wy_s.at[0], wy_r.at[yh]).wait_recv()
        shards_of = wyin[pl.ds(pl.multiple_of(yh * run16, run16), run16), :]
        w_block = w_rows(yh, my_x, core)
        w_block[:, 0 : s.kept] = mm(pick, shards_of).astype(BF16)
        if s.fold:
            w_block[:, s.kept :] = sum(
                mm(one_hot(wide, table[5 + k : 6 + k, : s.yl * ROWS16]), shards_of[:, k * s.fold : (k + 1) * s.fold])
                for k in range(3)
            ).astype(BF16)
        others(s.x, my_x, lambda x, yh=yh: wx_copy(yh, x, my_x).start())
        wc_copy(yh, my_x, core).start()

    first_turn(0)

    def unpack(c):
        first_2[c].wait()
        place_in = rt if Y_FIRST[c] else rt_q
        packed[:, s.cols[c]] = mm(place_in[...], b_in[c][...], TN).astype(BF16)

    def pass_on(step):
        yh = (my_yh + step) % s.yh

        def one(x):
            wx_copy(yh, x, x).wait_recv()
            wc_copy(yh, x, core).start()

        others(s.x, my_x, one)

    unpack(1)
    for step in range(s.yh - 1):
        pass_on(step)
    unpack(0)
    unpack(2)
    pass_on(s.yh - 1)
    unpack(3)

    def by_rows(step_rows, body):
        def step(i, carry):
            body(pl.ds(pl.multiple_of(i * step_rows, step_rows), step_rows))
            return carry

        lax.fori_loop(0, s.slots // step_rows, step, 0)

    def norm(rows):
        values = packed[rows, :].astype(F32)
        centered = values - jnp.mean(values, axis=1, keepdims=True)
        variance = jnp.mean(centered * centered, axis=1, keepdims=True)
        inverse = lax.rsqrt(variance + EPSILON)
        unit = centered * inverse
        inv[rows, :] = inverse
        standard[rows, :] = unit
        audio = jnp.broadcast_to(aud[rows, :], unit.shape) > 0.5
        gain = jnp.where(audio, gains[1:2, :], gains[0:1, :])
        bias = jnp.where(audio, biases[1:2, :], biases[0:1, :])
        normed[rows, :] = (unit * gain + bias).astype(BF16)

    by_rows(NORM_ROWS, norm)
    for h in range(2):
        normed_p[h] = mm(normed[...], feat[:, h * s.half : (h + 1) * s.half]).astype(BF16)

    def wc_all(body):
        for x in range(s.x):
            for yh in range(s.yh):
                body(wc_copy(yh, x, other))

    wc_all(lambda copy: copy.wait_recv())

    def project(i, carry):
        cols = pl.ds(pl.multiple_of(i * s.inner, LANES), s.inner)
        qkv[:, cols] = mm(normed[...], weight[:, cols]).astype(BF16)
        return carry

    lax.fori_loop(0, 3, project, 0, unroll=True)

    pair = 2 * HEAD_DIM
    scaling = 1.0 / HEAD_DIM**0.5

    def heads(i, carry):
        def part(k):
            return pl.ds(pl.multiple_of(k * s.inner + i * pair, LANES), pair)

        lane = lax.broadcasted_iota(jnp.int32, (1, pair), 1)
        masks = [jnp.where(lane < HEAD_DIM, 1.0, 0.0), jnp.where(lane < HEAD_DIM, 0.0, 1.0)]
        q, k, v, do = qkv[:, part(0)], qkv[:, part(1)], qkv[:, part(2)], dout[:, part(0)]

        def split(a):
            return [a * m.astype(BF16) for m in masks]

        qs, ks, vs, dos = split(q), split(k), split(v), split(do)
        probs = []
        for a in range(2):
            scores = mm(qs[a], k, NT) * scaling + same[...]
            exponent = jnp.exp(scores - jnp.max(scores, axis=1, keepdims=True))
            probs.append((exponent * (1.0 / jnp.sum(exponent, axis=1, keepdims=True))).astype(BF16))
        out = mm(jnp.concatenate(probs, axis=1), jnp.concatenate(vs, axis=0)).astype(BF16)
        attended[:, part(0)] = out
        delta = do.astype(F32) * out.astype(F32)
        grads = []
        for a in range(2):
            row_delta = jnp.sum(delta * masks[a], axis=1, keepdims=True)
            grad_probs = mm(dos[a], v, NT)
            grads.append((probs[a].astype(F32) * (grad_probs - row_delta) * scaling).astype(BF16))
        gqkv[:, part(0)] = mm(
            jnp.concatenate(grads, axis=1), jnp.concatenate(ks, axis=0)
        ).astype(BF16)
        gqkv[:, part(1)] = mm(
            jnp.concatenate(grads, axis=0), jnp.concatenate(qs, axis=0), TN
        ).astype(BF16)
        gqkv[:, part(2)] = mm(
            jnp.concatenate(probs, axis=0), jnp.concatenate(dos, axis=0), TN
        ).astype(BF16)
        return carry

    lax.fori_loop(0, s.inner // pair, heads, 0, unroll=True)
    stores = []

    def keep(src, dst):
        copy = pltpu.make_async_copy(src, dst, store.at[len(stores)])
        copy.start()
        stores.append(copy)

    keep(attended, attended_h)

    third = s.columns // 3

    def third_rows(k):
        return pl.ds(k * third, third)

    def gc_copy(k):
        return remote(g_send.at[third_rows(k), :], g_in.at[third_rows(k), :], gc_s.at[k], gc_r.at[k], sibling)

    for k in range(3):
        g_send[third_rows(k), :] = mm(gqkv[:, k * third : (k + 1) * third], normed_p[other], TN).astype(BF16)
        gc_copy(k).start()
        ends.append(gc_copy(k).wait_send)

    for k in range(3):
        rows = slice(k * s.width // 3, (k + 1) * s.width // 3)
        gnorm[:, rows] = mm(gqkv[...], weight[rows, :], NT)
    def piece_rows(p):
        return pl.ds(pl.multiple_of(p * s.chip_block, ROWS16), s.chip_block)

    def gx_copy(yh, x, slot):
        return remote(x_out.at[piece_rows(yh * s.x + x), :], x_in.at[yh, slot], gx_s.at[yh], gx_r.at[yh], at_x(x))

    sent = 0
    for k in range(3):
        g_own[third_rows(k), :] = mm(gqkv[:, k * third : (k + 1) * third], normed_p[core], TN)
        gc_copy(k).wait_recv()
        both = g_own[third_rows(k), :] + g_in[third_rows(k), :].astype(F32)
        g_own[third_rows(k), :] = both
        x_out[third_rows(k), :] = both.astype(BF16)
        while (sent + 1) * s.chip_block <= (k + 1) * third:
            yh, x = sent // s.x, sent % s.x

            @pl.when(x != my_x)
            def _(yh=yh, x=x):
                gx_copy(yh, x, my_x).start()

            sent += 1
    gx_all = []
    for yh in range(s.yh):
        part = x_in.at[yh, pl.ds(0, s.x - 1)]
        gx_all.append(remote(part, part, gx_s.at[yh], gx_r.at[yh], at_x((my_x + 1) % s.x)))
        ends.append(gx_all[yh].wait_send)

    my_za, my_zb = my_z // s.zb, my_z % s.zb
    n_zb[my_zb] = jnp.zeros_like(n_zb[0])

    def unnorm(rows):
        grad = gnorm[rows, :]
        unit = standard[rows, :]
        audio = jnp.broadcast_to(aud[rows, :], unit.shape) > 0.5
        gain = jnp.where(audio, gains[1:2, :], gains[0:1, :])
        gain_term = grad * unit
        n_zb[my_zb] += jnp.concatenate(
            [
                jnp.sum(jnp.where(audio, 0.0, gain_term), axis=0, keepdims=True),
                jnp.sum(jnp.where(audio, gain_term, 0.0), axis=0, keepdims=True),
                jnp.sum(jnp.where(audio, 0.0, grad), axis=0, keepdims=True),
                jnp.sum(jnp.where(audio, grad, 0.0), axis=0, keepdims=True),
            ],
            axis=0,
        )
        scaled = grad * gain
        out = inv[rows, :] * (
            scaled
            - jnp.mean(scaled, axis=1, keepdims=True)
            - unit * jnp.mean(scaled * unit, axis=1, keepdims=True)
        )
        gpacked[rows, :] = out.astype(BF16)

    by_rows(UNNORM_ROWS, unnorm)

    def total(buf, count):
        result = buf[0]
        for k in range(1, count):
            result = result + buf[k]
        return result

    class Sum:
        def __init__(self, buf, count, me, send, recv, at):
            self.buf, self.count, self.me, self.at = buf, count, me, at
            self.send, self.recv = send.at[0], recv.at[0]

        def start(self, value=None):
            if value is not None:
                self.buf[self.me] = value
            mine = self.buf.at[self.me]
            others(self.count, self.me, lambda p: remote(mine, mine, self.send, self.recv, self.at(p)).start())
            ends.append(self.whole().wait_send)

        def whole(self):
            part = self.buf.at[pl.ds(0, self.count - 1)]
            return remote(part, part, self.send, self.recv, self.at((self.me + 1) % self.count))

        def result(self):
            self.whole().wait_recv()
            return total(self.buf, self.count)

    sum_zb = Sum(n_zb, s.zb, my_zb, nzb_s, nzb_r, lambda zb: at_z(my_za * s.zb + zb))
    sum_za = Sum(n_za, s.za, my_za, nza_s, nza_r, lambda za: at_z(za * s.zb + my_zb))
    sum_c = Sum(n_c, s.c, core, nc_s, nc_r, lambda c: (grp_of(my_yh, my_x, c), f))
    sum_y = Sum(n_y, s.y, my_y, ny_s, ny_r, at_y)
    sum_x = Sum(n_x, s.x, my_x, nx_s, nx_r, at_x)
    sum_zb.start()

    for c in (1, 0, 2, 3):
        place_in = rt_q if Y_FIRST[c] else rt
        r_out[c][...] = mm(place_in[...], gpacked[:, s.back_cols[c]]).astype(BF16)
        if c < 2:
            back_1[c].start()

    def back_turn(c):
        back_1[c].wait()
        t_out[c][...] = turned(c, r_in[c][...])
        back_2[c].start()

    sum_c.start(sum_zb.result())
    back_turn(1)
    back_1[2].start()
    back_1[3].start()
    sum_x.start(sum_c.result())

    spread = one_hot(s.half, table[1:2, : s.yl * LANES])
    gy = Exchange(y_out, y_in, s.chip_block, s.y, my_y, gy_s.at[0], gy_r.at[0], at_y)
    for yh in range(s.yh):
        gx_all[yh].wait_recv()
        piece = g_own[piece_rows(yh * s.x + my_x), :]
        for step in range(1, s.x):
            piece = piece + x_in[yh, (my_x + step) % s.x].astype(F32)
        wide_piece = mm(piece.astype(BF16), spread).astype(BF16)
        for yl in range(s.yl):
            at = (yh * s.yl + yl) * s.chip_block
            y_out[at : at + s.chip_block, :] = wide_piece[:, yl * LANES : (yl + 1) * LANES]
            gy.start_one(yh * s.yl + yl)
    gy.started()
    back_turn(2)
    sum_za.start(sum_x.result())
    back_turn(3)
    back_turn(0)

    gy.wait()
    piece = y_in[0 : s.chip_block, :].astype(F32)
    for y in range(1, s.y):
        piece = piece + y_in[y * s.chip_block : (y + 1) * s.chip_block, :].astype(F32)
    apart = one_hot(s.z * ROWS8, table[4:5, :LANES])
    z_out[...] = mm(apart, piece.astype(BF16), NT)
    gz = Exchange(z_out, z_in, ROWS8, s.z, my_z, gz_s.at[0], gz_r.at[0], at_z)
    gz.start()
    sum_y.start(sum_za.result())

    def home(c):
        back_2[c].wait()
        grad_tokens[c][...] = mm((pt if Y_FIRST[c] else pt_q)[...], t_in[c][...]).astype(BF16)
        cols = s.back_cols[c]
        keep(grad_tokens[c], grad_tokens_h.at[:, pl.ds(cols.start, cols.stop - cols.start)])

    home(0)
    home(1)
    home(2)

    @pl.when(my_z == g)
    def _():
        part = weight.at[pl.ds(0, (s.z - 1) * ROWS16), pl.ds(0, s.kept)]
        remote(part, part, wz_s.at[0], wz_r.at[0], at_z((my_z + 1) % s.z)).wait_send()

    others(s.x, my_x, lambda x: [wx_copy(yh, x, my_x).wait_send() for yh in range(s.yh)])
    wc_all(lambda copy: copy.wait_send())
    for wait in ends[:-2]:
        wait()
    last_ends = ends[-2:]
    del ends[:]
    gz.wait()
    own = z_in[0:ROWS8, :]
    for z in range(1, s.z):
        own = own + z_in[z * ROWS8 : (z + 1) * ROWS8, :]
    f_send[...] = own
    f_copy = remote(f_send, f_in, gf_s.at[0], gf_r.at[0], sibling)
    f_copy.start()
    ends.append(f_copy.wait_send)
    home(3)
    norms = sum_y.result()
    grad_scale[...] = norms[0:2]
    grad_shift[...] = norms[2:4]
    keep(grad_scale, grad_scale_h)
    keep(grad_shift, grad_shift_h)
    f_copy.wait_recv()
    first = core == 0
    theirs = f_in[...]
    low, high = jnp.where(first, own, theirs), jnp.where(first, theirs, own)
    for at, value in ((0, low), (s.half_rows, high)):
        mine = jnp.where(first, value[:, : s.col_block], value[:, s.col_block :])
        grad_weight[at : at + s.half_rows, :] = mine[: s.half_rows]
    keep(grad_weight, grad_weight_h)

    for wait in last_ends + ends:
        wait()
    for copy in stores:
        copy.wait()


def copy_out(*refs):
    count = (len(refs) - 2) // 3
    sources, targets, held = refs[:count], refs[count : 2 * count], refs[2 * count : 3 * count]
    load, store = refs[3 * count :]
    loads = [pltpu.make_async_copy(sources[i], held[i], load.at[i]) for i in range(count)]
    stores = [pltpu.make_async_copy(held[i], targets[i], store.at[i]) for i in range(count)]
    for copy in loads:
        copy.start()
    for i in range(count):
        loads[i].wait()
        stores[i].start()
    for copy in stores:
        copy.wait()


def shards(
    tokens, send_order, recv_order, row_ids, frames, norm_scale, norm_shift, qkv_weight, d_out
):
    slots, width = tokens.shape
    columns = qkv_weight.shape[1]
    s = Sizes(lax.axis_size("grp"), lax.axis_size("fsdp"), slots, width, columns)
    whole = pl.BlockSpec(memory_space=pl.ANY)
    vm, dma = pltpu.VMEM, pltpu.SemaphoreType.DMA
    there, back = (
        [vm((slots, cols.stop - cols.start), BF16) for cols in parts] for parts in (s.cols, s.back_cols)
    )
    norms = (4, width)
    args = (
        tokens, send_order, recv_order, row_ids, frames, norm_scale, norm_shift, qkv_weight, d_out,
        jnp.asarray(index_rows(s)),
    )
    sds = jax.ShapeDtypeStruct
    outs = (
        sds((slots, s.inner), BF16), sds((slots, width), BF16),
        sds((s.rows, s.col_block), F32), sds((2, width), F32), sds((2, width), F32),
    )
    scratch = [vm(a.shape, a.dtype) for a in args]
    scratch += [vm((slots, s.inner), BF16), back]
    scratch += [vm(a.shape, a.dtype) for a in outs[2:]]
    scratch += [
        vm((slots, slots), BF16), vm((slots, slots), BF16), vm((slots, slots), BF16),
        vm((slots, slots), BF16), vm((slots, slots), BF16),
        vm((width, width), BF16), there, there, there, there, vm((slots, width), BF16),
        vm((ROWS16, s.kept), BF16), vm((ROWS16, s.kept), BF16),
        vm((s.y * ROWS16, s.kept), BF16), vm((width, columns), BF16),
        vm((slots, 1), F32), vm((slots, slots), F32), vm((slots, width), F32), vm((slots, 1), F32),
        vm((slots, width), BF16), vm((2, slots, s.half), BF16),
        vm((slots, columns), BF16), vm((slots, columns), BF16),
        vm((slots, width), F32), vm((slots, width), BF16),
        back, back, back, back,
        vm((columns, s.half), BF16), vm((columns, s.half), F32), vm((columns, s.half), BF16),
        vm((columns, s.half), BF16), vm((s.yh, s.x, s.chip_block, s.half), BF16),
        vm((s.y * s.chip_block, LANES), BF16), vm((s.y * s.chip_block, LANES), BF16),
        vm((s.z * ROWS8, s.chip_block), F32), vm((s.z * ROWS8, s.chip_block), F32),
        vm((ROWS8, s.chip_block), F32), vm((ROWS8, s.chip_block), F32),
        vm((s.c,) + norms, F32), vm((s.x,) + norms, F32), vm((s.y,) + norms, F32),
        vm((s.zb,) + norms, F32), vm((s.za,) + norms, F32),
    ]
    xy = s.x * s.yh
    counts = [len(args), len(outs) + CHUNKS - 1]
    counts += [CHUNKS] * 8
    counts += [1, 1, 1, s.yh, xy, xy, xy, xy]
    counts += [3, 3, s.yh, s.yh] + [1] * 6
    counts += [1] * 10
    scratch += [dma((n,)) for n in counts]
    results = pl.pallas_call(
        functools.partial(kernel, s),
        out_shape=outs,
        in_specs=[whole] * len(args),
        out_specs=(whole,) * len(outs),
        scratch_shapes=scratch,
        compiler_params=pltpu.CompilerParams(
            collective_id=0, has_side_effects=True, vmem_limit_bytes=56 * 1024 * 1024
        ),
        cost_estimate=pl.CostEstimate(
            flops=2_000_000_000, bytes_accessed=3_000_000, transcendentals=400_000
        ),
        name="joint_block",
    )(*args)
    return pl.pallas_call(
        copy_out,
        out_shape=outs,
        in_specs=[whole] * len(outs),
        out_specs=(whole,) * len(outs),
        scratch_shapes=[vm(a.shape, a.dtype) for a in outs] + [dma((len(outs),))] * 2,
        name="copy_out",
    )(*results)


def solution(mesh):
    rows = P(("grp", "fsdp"), None)
    return jax.shard_map(
        shards,
        mesh=mesh,
        in_specs=(rows, rows, rows, rows, rows, P(), P(), P("fsdp", None), rows),
        out_specs=(rows, rows, P("fsdp", "grp"), P(), P()),
        check_vma=False,
    )
```
